128 devices in a mesh: blk: 16 (over x_lo, z, core), grp: 8 (over y, x_hi).
Axes of the slice: x: 4 (x_hi: 2, x_lo: 2; x = x_hi * 2 + x_lo), y: 4, z: 4, core: 2. Of those that a mesh axis runs over, the one named last changes fastest.
Arguments:
- block_values: bfloat16 [6144, 16, 64, 64], P('blk', 'grp'), may hold values from -1.5 to 1.5
- block_columns: int32 [6144, 16], P('blk', 'grp'), may hold values from 0 to 6143, as said below
- row_counts: int32 [6144], P('blk'), may hold values from 6 to 16
- prolong_blocks: bfloat16 [6144, 64, 64], P(('blk', 'grp')), may hold values from -0.75 to 0.75
- aggregates: int32 [6144], P(('blk', 'grp')), may hold values from 0 to 63, as said below
Outputs:
- coarse_blocks: float32 [64, 64, 64, 64], P('grp', 'blk')
The draws below stay inside these ranges and needn't reach their ends.
Inputs may be any that keep to these rules, and one draw needn't show every extreme that they name: `aggregates`: the aggregate of a fine block row of panel p, rows p * 384 to (p + 1) * 384 - 1, lies in p * 4 to (p + 1) * 4 - 1. `block_columns`: A block column of a row of panel p lies in a panel p + d modulo the number of panels, for some d of -2 to 2; slot 0 of each row holds the row itself.
All inputs are finite; a program needn't handle non-finite values.
Results may differ from the reference program's by a relative error of at most 0.0029.
Values may be sent and summed in bfloat16 or wider, within the bound.
A program may use at most 192 MiB of HBM per device.

```python
import jax
import jax.numpy as jnp
from jax import lax

BS = 64
K = 16
CB = 4
RBG = 48
RB = 384
NB = 6144
N_BLK = 16
N_GRP = 8


def draw_aggregates(key, part):
    positions = jnp.arange(NB, dtype=jnp.int32)
    panel = positions // RB
    within = positions % RB
    picked = jax.random.randint(key, (NB,), 0, CB, dtype=jnp.int32)
    picked = jnp.where(within == 0, 0, picked)
    picked = jnp.where(within == RB - 1, CB - 1, picked)
    return (panel * CB + picked).astype(jnp.int32)


def draw_block_columns(key, part):
    key_offset = jax.random.fold_in(key, 11)
    key_within = jax.random.fold_in(key, 12)
    rows = jnp.arange(NB, dtype=jnp.int32)[:, None]
    slots = jnp.arange(K, dtype=jnp.int32)[None, :]
    panel = rows // RB
    offset = jax.random.randint(key_offset, (NB, K), -2, 3, dtype=jnp.int32)
    within = jax.random.randint(key_within, (NB, K), 0, RB, dtype=jnp.int32)
    panels_total = NB // RB
    columns = jnp.mod(panel + offset, panels_total) * RB + within
    columns = jnp.where(slots == 0, rows, columns)
    corner = jnp.logical_and(rows == 0, slots == K - 1)
    columns = jnp.where(corner, NB - 1, columns)
    return columns.astype(jnp.int32)


def touch_ends(result, rng, smallest, largest):
    index_at = [jax.random.randint(jax.random.fold_in(rng, axis), (), 0, length) for axis, length in enumerate(result.shape)]
    widest = result.shape.index(max(result.shape))
    next_to = index_at[:widest] + [(index_at[widest] + 1) % result.shape[widest]] + index_at[widest + 1:]
    return result.at[tuple(index_at)].set(smallest).at[tuple(next_to)].set(largest)


def levels(own_key, dims, split, low, high):
    factor_of = 1.0
    for dim, blocks in split:
        steps = jax.random.uniform(jax.random.fold_in(jax.random.fold_in(own_key, 6), dim), (blocks,), jnp.float32, low / len(split), high / len(split))
        factor_of = factor_of * jnp.repeat(jnp.exp(steps), dims[dim] // blocks).reshape((-1,) + (1,) * (len(dims) - 1 - dim))
    return factor_of


def centred(key, extent, width, reach, cuts=(), kind=jnp.bfloat16):
    drawn = width * jax.random.normal(key, extent, jnp.float32)
    if cuts:
        drawn = drawn * levels(key, extent, cuts, -0.22, 0.18)
    return jnp.clip(drawn, -reach, reach).astype(kind)


def setup_inputs(seed: int = 0) -> dict:
    arg_keys = jax.random.split(jax.random.key(seed), 6)
    block_values = centred(arg_keys[0], (NB, K, BS, BS), 0.25, 1.5, ((0, 16), (1, 8)))
    block_columns = draw_block_columns(jax.random.fold_in(arg_keys[5], 71), 0)
    row_counts = touch_ends(jax.random.randint(arg_keys[2], (NB,), 6, K + 1), jax.random.fold_in(arg_keys[2], 1), 6, K).astype(jnp.int32)
    prolong_blocks = centred(arg_keys[3], (NB, BS, BS), BS ** -0.5, 0.75, ((0, 128),))
    aggregates = draw_aggregates(jax.random.fold_in(arg_keys[5], 71), 0)
    return {"block_values": block_values, "block_columns": block_columns, "row_counts": row_counts, "prolong_blocks": prolong_blocks, "aggregates": aggregates}


def reference(block_values, block_columns, row_counts, prolong_blocks, aggregates):
    panel_rows = RBG * N_GRP
    coarse_count = CB * N_BLK
    slot_index = jnp.arange(K, dtype=jnp.int32)

    def panel_step(accumulated, panel):
        start = (panel * panel_rows).astype(jnp.int32)
        values = lax.dynamic_slice_in_dim(block_values, start, panel_rows, 0).astype(jnp.float32)
        columns = lax.dynamic_slice_in_dim(block_columns, start, panel_rows, 0)
        counts_here = lax.dynamic_slice_in_dim(row_counts, start, panel_rows, 0)
        own_blocks = lax.dynamic_slice_in_dim(prolong_blocks, start, panel_rows, 0).astype(jnp.float32)
        own_aggs = lax.dynamic_slice_in_dim(aggregates, start, panel_rows, 0)
        picked = jnp.take(prolong_blocks, columns, axis=0).astype(jnp.float32)
        picked_aggs = jnp.take(aggregates, columns, axis=0)
        product = jnp.einsum('rkab,rkbc->rkac', values, picked)
        live = slot_index[None, :] < counts_here[:, None]
        product = jnp.where(live[:, :, None, None], product, 0.0).astype(jnp.bfloat16)
        product = lax.optimization_barrier(product).astype(jnp.float32)
        restricted = jnp.einsum('rba,rkbc->rkac', own_blocks, product)
        target = picked_aggs * coarse_count + own_aggs[:, None]
        accumulated = accumulated.at[target.reshape(-1)].add(restricted.reshape(-1, BS, BS))
        return accumulated, None

    total = jnp.zeros((coarse_count * coarse_count, BS, BS), jnp.float32)
    total, _ = lax.scan(panel_step, total, jnp.arange(N_BLK, dtype=jnp.int32))
    return total.reshape(coarse_count, coarse_count, BS, BS)
```

```python
import functools

import jax
import jax.numpy as jnp
from jax import lax
from jax.experimental import pallas as pl
from jax.experimental.pallas import tpu as pltpu
from jax.sharding import PartitionSpec as P

MESH = pl.DeviceIdType.MESH
BF16, F32 = jnp.bfloat16, jnp.float32

BS = 64
CB = 4
ROWS = 384
SHARD = 48
PAIRS = SHARD // 2
PANELS = 16
GROUP = 8
SPAN = 5
HEAD = 16
LEN = HEAD + PAIRS * BS
CUT = HEAD + 14 * BS
F_PART, L_PART = (0, CUT), (CUT, LEN - CUT)
F_HALVES = ((0, 448), (448, CUT - 448))
L_HALVES = ((CUT, 320), (CUT + 320, 320))
SLOTS = 2
TARGETS = SPAN * CB * CB * 2
ACCS = TARGETS + 8
BLOCKS = TARGETS // 4
SHARE = BLOCKS // GROUP


def gather_kernel(p_ref, agg_ref, win_ref, raw, own, local_sem, send_sem, recv_sem):
    b, g = lax.axis_index("blk"), lax.axis_index("grp")
    core = b % 2
    y, h = g // 2, g % 2
    up_k, down_k = ((b + 2) % PANELS, g), ((b + PANELS - 2) % PANELS, g)
    up_y, down_y = (b, (g + 2) % GROUP), (b, (g + GROUP - 2) % GROUP)
    across, sibling = (b, g + 1 - 2 * h), (b + 1 - 2 * core, g)

    load = pltpu.make_async_copy(p_ref, raw, local_sem.at[0])
    load.start()
    barrier = pltpu.get_barrier_semaphore()
    for device in (up_k, down_k, up_y, down_y, across, sibling):
        pl.semaphore_signal(barrier, inc=1, device_id=device, device_id_type=MESH)
    load.wait()
    own[0:HEAD, :] = agg_ref[...]

    def pack(j, carry):
        row = pl.multiple_of(HEAD + j * BS, HEAD)
        own[pl.ds(row, BS), :] = jnp.concatenate([raw[2 * j], raw[2 * j + 1]], axis=-1)
        return carry

    lax.fori_loop(0, PAIRS, pack, 0)
    keep = pltpu.make_async_copy(own, win_ref.at[2, g], local_sem.at[1])
    keep.start()
    pl.semaphore_wait(barrier, 6)

    copies = {}

    def at(d, dy, dh):
        return win_ref.at[d, ((y + dy) % 4) * 2 + (h + dh) % 2]

    def send(name, part, d, dy, dh, to_d, device, src=None):
        start, size = part
        piece = pl.ds(start, size)
        n = len(copies)
        source = own if src is not None else at(d, dy, dh)
        copies[name] = pltpu.make_async_remote_copy(
            src_ref=source.at[piece, :],
            dst_ref=at(to_d, dy, dh).at[piece, :],
            send_sem=send_sem.at[n],
            recv_sem=recv_sem.at[n],
            device_id=device,
            device_id_type=MESH,
        )
        copies[name].start()

    def got(*names):
        for name in names:
            copies[name].wait_recv()

    def to_y(part, tag, d, dh, src=None):
        send((tag, "y+", d, dh), part, d, 0, dh, d, up_y, src)
        send((tag, "y-", d, dh), part, d, 0, dh, d, down_y, src)

    def on_y(halves, tag, d, dh):
        send((tag, "f+", d, dh), halves[0], d, -1, dh, d, up_y)
        send((tag, "f-", d, dh), halves[1], d, 1, dh, d, down_y)

    def to_z(part, tag, dy, dh, src=None):
        send((tag, "z+", dy, dh), part, 2, dy, dh, 0, up_k, src)
        send((tag, "z-", dy, dh), part, 2, dy, dh, 4, down_k, src)

    def over(part, tag, dy, dh, src=None):
        send((tag, "s", dy, dh), part, 2, dy, dh, 1 + 2 * core, sibling, src)

    def over_far(part, tag, dy, dh):
        send((tag, "t", dy, dh), part, 4 - 4 * core, dy, dh, 3 - 2 * core, sibling)

    send(("F", "x"), F_PART, 2, 0, 0, 2, across, own)
    to_y(F_PART, "F", 2, 0, own)
    to_z(F_PART, "F", 0, 0, own)
    send(("L", "x"), L_PART, 2, 0, 0, 2, across, own)
    to_z(L_PART, "L", 0, 0, own)
    to_y(L_PART, "L", 2, 0, own)
    over((0, LEN), "A", 0, 0, own)

    got(("F", "x"))
    to_y(F_PART, "F", 2, 1)
    to_z(F_PART, "F", 0, 1)
    got(("F", "y+", 2, 0), ("F", "y-", 2, 0))
    on_y(F_HALVES, "F", 2, 0)
    for dy in (-1, 1):
        to_z(F_PART, "F", dy, 0)
    got(("L", "x"))
    to_z(L_PART, "L", 0, 1)
    to_y(L_PART, "L", 2, 1)
    over((0, LEN), "A", 0, 1)
    got(("L", "y+", 2, 0), ("L", "y-", 2, 0))
    on_y(L_HALVES, "L", 2, 0)
    for dy in (-1, 1):
        over((0, LEN), "A", dy, 0)
    got(("L", "z+", 0, 0), ("L", "z-", 0, 0))
    for d in (0, 4):
        to_y(L_PART, "L", d, 0)
    over_far(L_PART, "L", 0, 0)
    got(("F", "y+", 2, 1), ("F", "y-", 2, 1))
    on_y(F_HALVES, "F", 2, 1)
    for dy in (-1, 1):
        to_z(F_PART, "F", dy, 1)
    got(("F", "f+", 2, 0), ("F", "f-", 2, 0))
    to_z(F_PART, "F", 2, 0)
    got(("L", "z+", 0, 1), ("L", "z-", 0, 1))
    for d in (0, 4):
        to_y(L_PART, "L", d, 1)
    over_far(L_PART, "L", 0, 1)
    got(("F", "f+", 2, 1), ("F", "f-", 2, 1))
    to_z(F_PART, "F", 2, 1)
    got(("L", "y+", 2, 1), ("L", "y-", 2, 1))
    on_y(L_HALVES, "L", 2, 1)
    for dy in (-1, 1):
        over((0, LEN), "A", dy, 1)
    got(("L", "f+", 2, 0), ("L", "f-", 2, 0))
    over((0, LEN), "A", 2, 0)
    got(("F", "z+", 0, 0), ("F", "z-", 0, 0))
    over_far(F_PART, "F", 0, 0)
    for d in (0, 4):
        got(("L", "y+", d, 0), ("L", "y-", d, 0))
        on_y(L_HALVES, "L", d, 0)
    for dy in (-1, 1):
        over_far(L_PART, "L", dy, 0)
    got(("L", "f+", 2, 1), ("L", "f-", 2, 1))
    over((0, LEN), "A", 2, 1)
    got(("F", "z+", 0, 1), ("F", "z-", 0, 1))
    over_far(F_PART, "F", 0, 1)
    for dy in (-1, 1):
        got(("F", "z+", dy, 0), ("F", "z-", dy, 0))
        over_far(F_PART, "F", dy, 0)
    for d in (0, 4):
        got(("L", "y+", d, 1), ("L", "y-", d, 1))
        on_y(L_HALVES, "L", d, 1)
    for dy in (-1, 1):
        over_far(L_PART, "L", dy, 1)
    for dy, dh in ((-1, 1), (1, 1), (2, 0), (2, 1)):
        got(("F", "z+", dy, dh), ("F", "z-", dy, dh))
        over_far(F_PART, "F", dy, dh)
    for dh in (0, 1):
        for d in (0, 4):
            got(("L", "f+", d, dh), ("L", "f-", d, dh))
        over_far(L_PART, "L", 2, dh)
    for name in copies:
        if name[1] in ("s", "t"):
            got(name)
    for copy in copies.values():
        copy.wait_send()
    keep.wait()


COPIES = 86 - 8


def gathered(prolong, aggs):
    return pl.pallas_call(
        gather_kernel,
        out_shape=jax.ShapeDtypeStruct((SPAN, GROUP, LEN, 2 * BS), BF16),
        in_specs=[
            pl.BlockSpec(memory_space=pl.ANY),
            pl.BlockSpec(memory_space=pltpu.VMEM),
        ],
        out_specs=pl.BlockSpec(memory_space=pl.ANY),
        scratch_shapes=[
            pltpu.VMEM((SHARD, BS, BS), BF16),
            pltpu.VMEM((LEN, 2 * BS), BF16),
            pltpu.SemaphoreType.DMA((2,)),
            pltpu.SemaphoreType.DMA((COPIES,)),
            pltpu.SemaphoreType.DMA((COPIES,)),
        ],
        compiler_params=pltpu.CompilerParams(collective_id=0, has_side_effects=True),
        name="gather_window",
    )(prolong, aggs)


def compute_kernel(
    row_ref, loc_ref, base_ref, tj_ref, a_ref, win_ref, part_ref, turned, blocks, acc
):
    def clear(t, carry):
        acc[t] = jnp.zeros((BS, 2 * BS), F32)
        return carry

    lax.fori_loop(0, ACCS, clear, 0)

    for first in range(0, ROWS, 128):

        def turn(r, carry, first=first):
            both = jnp.concatenate(
                [a_ref[s, r, :, first : first + 128] for s in range(SLOTS)], axis=0
            )
            turned[pl.ds(pl.multiple_of(r * 128, 128), 128), :] = both.astype(F32).T
            return carry

        lax.fori_loop(0, BS, turn, 0, unroll=4)

        def collect(i, carry, first=first):
            blocks[first + i] = turned[pl.ds(i, BS, stride=128), :].astype(BF16)
            return carry

        lax.fori_loop(0, 128, collect, 0, unroll=8)

    for shard in range(GROUP):

        def left(j, carry, shard=shard):
            start = (2 * GROUP + shard) * LEN + HEAD + j * BS
            both = win_ref[pl.ds(pl.multiple_of(start, HEAD), BS), :].T
            for half in range(2):
                i = shard * SHARD + 2 * j + half
                t = jnp.dot(
                    both[half * BS : (half + 1) * BS, :],
                    blocks[i],
                    preferred_element_type=F32,
                )
                blocks[i] = t.astype(BF16)
            return carry

        lax.fori_loop(0, PAIRS, left, 0, unroll=4)

    def right(i, carry):
        t = blocks[i]
        none = jnp.zeros((BS, 2 * BS), BF16)
        for s in range(SLOTS):
            row = pl.multiple_of(row_ref[s, i], HEAD)
            picked = win_ref[pl.ds(row, BS), :]
            stack = [picked, none] if s == 0 else [none, picked]
            r = jnp.dot(t, jnp.concatenate(stack, axis=0), preferred_element_type=F32)
            target = tj_ref[loc_ref[s, i]] + base_ref[s, i]
            acc[target] += r
        return carry

    lax.fori_loop(0, ROWS, right, 0, unroll=4)

    low = lax.broadcasted_iota(jnp.int32, (BS, 2 * BS), 1) < BS

    def fold(t, carry):
        one, two = acc[4 * t], acc[4 * t + 1]
        three, four = acc[4 * t + 2], acc[4 * t + 3]
        first = one + pltpu.roll(two, BS, 1)
        second = pltpu.roll(three, BS, 1) + four
        part_ref[t] = jnp.where(low, first, second)
        return carry

    lax.fori_loop(0, BLOCKS, fold, 0)


def computed(rows, locs, bases, tj, a, win):
    smem = pl.BlockSpec(memory_space=pltpu.SMEM)
    vmem = pl.BlockSpec(memory_space=pltpu.VMEM)
    return pl.pallas_call(
        compute_kernel,
        out_shape=jax.ShapeDtypeStruct((BLOCKS, BS, 2 * BS), F32),
        in_specs=[smem, smem, smem, smem, vmem, vmem],
        out_specs=vmem,
        scratch_shapes=[
            pltpu.VMEM((BS * 128, 128), F32),
            pltpu.VMEM((ROWS, BS, 2 * BS), BF16),
            pltpu.VMEM((ACCS, BS, 2 * BS), F32),
        ],
        compiler_params=pltpu.CompilerParams(vmem_limit_bytes=56 * 2**20),
        name="triple_products",
    )(rows, locs, bases, tj, a, win)


def reduce_kernel(part_ref, out_ref, landed, total, placed, send_sem, recv_sem, send2, recv2):
    b, g = lax.axis_index("blk"), lax.axis_index("grp")
    others = [(g + n) % GROUP for n in range(1, GROUP)]
    barrier = pltpu.get_barrier_semaphore()
    for other in others:
        pl.semaphore_signal(barrier, inc=1, device_id=(b, other), device_id_type=MESH)
    pl.semaphore_wait(barrier, GROUP - 1)
    first = []
    for n, other in enumerate(others):
        copy = pltpu.make_async_remote_copy(
            src_ref=part_ref.at[pl.ds(other * SHARE, SHARE)],
            dst_ref=landed.at[n],
            send_sem=send_sem.at[n],
            recv_sem=recv_sem.at[n],
            device_id=(b, other),
            device_id_type=MESH,
        )
        copy.start()
        first.append(copy)
    out_ref[...] = jnp.zeros(out_ref.shape, F32)
    total[...] = part_ref[pl.ds(g * SHARE, SHARE)]
    for n, copy in enumerate(first):
        copy.wait_recv()
        total[...] += landed[n]

    def owner(m):
        panel = (b + PANELS - 2 + m // 8) % PANELS
        return panel, panel // 2

    def hop(e, m, device):
        return pltpu.make_async_remote_copy(
            src_ref=total.at[e],
            dst_ref=placed.at[m],
            send_sem=send2.at[e],
            recv_sem=recv2.at[m],
            device_id=(b, device),
            device_id_type=MESH,
        )

    def keep(panel, m, block):
        row = (panel % 2) * CB + (m % 8) // 2
        column = (m % 2) * 2
        out_ref[row, column] = block[:, :BS]
        out_ref[row, column + 1] = block[:, BS:]

    for e in range(SHARE):
        m = g * SHARE + e
        panel, device = owner(m)

        @pl.when(device != g)
        def _(e=e, m=m, device=device):
            hop(e, m, device).start()

        @pl.when(device == g)
        def _(e=e, m=m, panel=panel):
            keep(panel, m, total[e])

    def arrive(m, carry):
        panel, device = owner(m)

        @pl.when(jnp.logical_and(device == g, m // SHARE != g))
        def _():
            hop(0, m, (g + 1) % GROUP).wait_recv()
            keep(panel, m, placed[m])

        return carry

    lax.fori_loop(0, BLOCKS, arrive, 0)
    for e in range(SHARE):
        m = g * SHARE + e
        panel, device = owner(m)

        @pl.when(device != g)
        def _(e=e, m=m, device=device):
            hop(e, m, device).wait_send()

    for copy in first:
        copy.wait_send()


def reduced(part):
    vmem = pl.BlockSpec(memory_space=pltpu.VMEM)
    return pl.pallas_call(
        reduce_kernel,
        out_shape=jax.ShapeDtypeStruct((GROUP, CB, BS, BS), F32),
        in_specs=[vmem],
        out_specs=vmem,
        scratch_shapes=[
            pltpu.VMEM((GROUP - 1, SHARE, BS, 2 * BS), F32),
            pltpu.VMEM((SHARE, BS, 2 * BS), F32),
            pltpu.VMEM((BLOCKS, BS, 2 * BS), F32),
            pltpu.SemaphoreType.DMA((GROUP - 1,)),
            pltpu.SemaphoreType.DMA((GROUP - 1,)),
            pltpu.SemaphoreType.DMA((SHARE,)),
            pltpu.SemaphoreType.DMA((BLOCKS,)),
        ],
        compiler_params=pltpu.CompilerParams(collective_id=1, has_side_effects=True),
        name="reduce_blocks",
    )(part)


def local(block_values, block_columns, row_counts, prolong_blocks, aggregates):
    b, g = lax.axis_index("blk"), lax.axis_index("grp")
    head = jnp.pad((aggregates % CB).astype(BF16)[None, :], ((0, HEAD - 1), (0, 2 * BS - SHARD)))
    win = gathered(prolong_blocks, head)

    loc = jnp.mod(block_columns.T - (b - 2) * ROWS, PANELS * ROWS)
    slot = g * SLOTS + jnp.arange(SLOTS, dtype=jnp.int32)
    live = slot[:, None] < row_counts[None, :]
    loc = jnp.where(live, loc, SPAN * ROWS)
    rows = (loc // SHARD) * LEN + HEAD + (loc % SHARD) // 2 * BS
    rows = jnp.where(live, rows, HEAD)

    near = win[:, :, 0, :SHARD].astype(jnp.int32).reshape(SPAN, ROWS)
    tj = (jnp.arange(SPAN, dtype=jnp.int32)[:, None] * CB + near) * (2 * CB)
    tj = jnp.concatenate([tj.reshape(-1), jnp.full((128,), TARGETS, jnp.int32)])
    bases = jnp.where(live, near[2][None, :] * 2 + loc % 2, 0)

    a = jnp.transpose(block_values, (1, 2, 3, 0))
    part = computed(rows, loc, bases, tj, a, win.reshape(-1, 2 * BS))
    return reduced(part)


def solution(mesh):
    in_specs = (
        P("blk", "grp", None, None),
        P("blk", "grp"),
        P("blk"),
        P(("blk", "grp"), None, None),
        P(("blk", "grp")),
    )
    out_specs = P("grp", "blk", None, None)
    return jax.shard_map(local, mesh=mesh, in_specs=in_specs, out_specs=out_specs, check_vma=False)
```

```python
import functools

import jax
import jax.numpy as jnp
from jax import lax
from jax.experimental import pallas as pl
from jax.experimental.pallas import tpu as pltpu
from jax.sharding import PartitionSpec as P

MESH = pl.DeviceIdType.MESH
BF16, F32 = jnp.bfloat16, jnp.float32

BS = 64
CB = 4
ROWS = 384
SHARD = 48
PAIRS = SHARD // 2
PANELS = 16
GROUP = 8
SPAN = 5
HEAD = 16
LEN = HEAD + PAIRS * BS
CUT = HEAD + 14 * BS
F_PART, L_PART = (0, CUT), (CUT, LEN - CUT)
F_HALVES = ((0, 448), (448, CUT - 448))
L_HALVES = ((CUT, 320), (CUT + 320, 320))
SLOTS = 2
TARGETS = SPAN * CB * CB * 2
ACCS = TARGETS + 8
BLOCKS = TARGETS // 4
SHARE = BLOCKS // GROUP
PITCH = 136


def turn(a_ref, turned, blocks, first):
    def over(r, carry):
        both = jnp.concatenate(
            [a_ref[s, r, :, first : first + 128] for s in range(SLOTS)], axis=0
        )
        start = pl.multiple_of(r * PITCH, 8)
        turned[pl.ds(start, 128), :] = both.T.astype(F32)
        return carry

    lax.fori_loop(0, BS, over, 0, unroll=16)

    def collect(i, carry):
        blocks[first + i] = turned[pl.ds(i, BS, stride=PITCH), :].astype(BF16)
        return carry

    lax.fori_loop(0, 128, collect, 0, unroll=16)


def left(win_ref, blocks, shard):
    def pair(j, carry):
        start = pl.multiple_of(HEAD + j * BS, HEAD)
        both = win_ref[2, shard, pl.ds(start, BS), :].T
        for half in range(2):
            i = shard * SHARD + 2 * j + half
            t = jnp.dot(
                both[half * BS : (half + 1) * BS, :], blocks[i], preferred_element_type=F32
            )
            blocks[i] = t.astype(BF16)
        return carry

    lax.fori_loop(0, PAIRS, pair, 0, unroll=12)


def gather_kernel(
    p_ref, agg_ref, columns_ref, counts_ref, a_hbm,
    win_ref, blocks, code_ref, table_ref,
    raw, own, a_ref, turned, local_sem, send_sem, recv_sem,
):
    b, g = lax.axis_index("blk"), lax.axis_index("grp")
    core = b % 2
    y, h = g // 2, g % 2
    up_k, down_k = ((b + 2) % PANELS, g), ((b + PANELS - 2) % PANELS, g)
    up_y, down_y = (b, (g + 2) % GROUP), (b, (g + GROUP - 2) % GROUP)
    across, sibling = (b, g + 1 - 2 * h), (b + 1 - 2 * core, g)

    load = pltpu.make_async_copy(p_ref, raw, local_sem.at[0])
    load.start()
    barrier = pltpu.get_barrier_semaphore()
    for device in (up_k, down_k, up_y, down_y, across, sibling):
        pl.semaphore_signal(barrier, inc=1, device_id=device, device_id_type=MESH)
    own[0:HEAD, :] = jnp.zeros((HEAD, 2 * BS), BF16)
    own[0:HEAD, 0:SHARD] = jnp.broadcast_to(
        (agg_ref[...] % CB).astype(F32), (HEAD, SHARD)
    ).astype(BF16)
    load.wait()
    load_a = pltpu.make_async_copy(a_hbm, a_ref, local_sem.at[2])
    load_a.start()

    def pack(j, carry):
        row = pl.multiple_of(HEAD + j * BS, HEAD)
        own[pl.ds(row, BS), :] = jnp.concatenate([raw[2 * j], raw[2 * j + 1]], axis=-1)
        return carry

    lax.fori_loop(0, PAIRS, pack, 0, unroll=8)
    keep = pltpu.make_async_copy(own, win_ref.at[2, g], local_sem.at[1])
    keep.start()
    pl.semaphore_wait(barrier, 6)

    copies = {}

    def at(d, dy, dh):
        return win_ref.at[d, ((y + dy) % 4) * 2 + (h + dh) % 2]

    def send(name, part, d, dy, dh, to_d, device, src=None):
        start, size = part
        piece = pl.ds(start, size)
        n = len(copies)
        source = own if src is not None else at(d, dy, dh)
        copies[name] = pltpu.make_async_remote_copy(
            src_ref=source.at[piece, :],
            dst_ref=at(to_d, dy, dh).at[piece, :],
            send_sem=send_sem.at[n],
            recv_sem=recv_sem.at[n],
            device_id=device,
            device_id_type=MESH,
        )
        copies[name].start()

    def got(*names):
        for name in names:
            copies[name].wait_recv()

    def to_y(part, tag, d, dh, src=None):
        send((tag, "y+", d, dh), part, d, 0, dh, d, up_y, src)
        send((tag, "y-", d, dh), part, d, 0, dh, d, down_y, src)

    def on_y(halves, tag, d, dh):
        send((tag, "f+", d, dh), halves[0], d, -1, dh, d, up_y)
        send((tag, "f-", d, dh), halves[1], d, 1, dh, d, down_y)

    def to_z(part, tag, dy, dh, src=None):
        send((tag, "z+", dy, dh), part, 2, dy, dh, 0, up_k, src)
        send((tag, "z-", dy, dh), part, 2, dy, dh, 4, down_k, src)

    def over(part, tag, dy, dh, src=None):
        send((tag, "s", dy, dh), part, 2, dy, dh, 1 + 2 * core, sibling, src)

    def over_far(part, tag, dy, dh):
        send((tag, "t", dy, dh), part, 4 - 4 * core, dy, dh, 3 - 2 * core, sibling)

    send(("F", "x"), F_PART, 2, 0, 0, 2, across, own)
    to_y(F_PART, "F", 2, 0, own)
    to_z(F_PART, "F", 0, 0, own)
    send(("L", "x"), L_PART, 2, 0, 0, 2, across, own)
    to_z(L_PART, "L", 0, 0, own)
    to_y(L_PART, "L", 2, 0, own)
    over((0, LEN), "A", 0, 0, own)

    load_a.wait()
    turn(a_ref, turned, blocks, 0)
    got(("F", "x"))
    to_y(F_PART, "F", 2, 1)
    to_z(F_PART, "F", 0, 1)
    got(("F", "y+", 2, 0), ("F", "y-", 2, 0))
    on_y(F_HALVES, "F", 2, 0)
    for dy in (-1, 1):
        to_z(F_PART, "F", dy, 0)
    got(("L", "x"))
    to_z(L_PART, "L", 0, 1)
    to_y(L_PART, "L", 2, 1)
    over((0, LEN), "A", 0, 1)
    got(("L", "y+", 2, 0), ("L", "y-", 2, 0))
    on_y(L_HALVES, "L", 2, 0)
    for dy in (-1, 1):
        over((0, LEN), "A", dy, 0)
    got(("L", "z+", 0, 0), ("L", "z-", 0, 0))
    for d in (0, 4):
        to_y(L_PART, "L", d, 0)
    over_far(L_PART, "L", 0, 0)
    turn(a_ref, turned, blocks, 128)
    got(("F", "y+", 2, 1), ("F", "y-", 2, 1))
    on_y(F_HALVES, "F", 2, 1)
    for dy in (-1, 1):
        to_z(F_PART, "F", dy, 1)
    got(("F", "f+", 2, 0), ("F", "f-", 2, 0))
    to_z(F_PART, "F", 2, 0)
    got(("L", "z+", 0, 1), ("L", "z-", 0, 1))
    for d in (0, 4):
        to_y(L_PART, "L", d, 1)
    over_far(L_PART, "L", 0, 1)
    got(("F", "f+", 2, 1), ("F", "f-", 2, 1))
    to_z(F_PART, "F", 2, 1)
    got(("L", "y+", 2, 1), ("L", "y-", 2, 1))
    on_y(L_HALVES, "L", 2, 1)
    for dy in (-1, 1):
        over((0, LEN), "A", dy, 1)
    turn(a_ref, turned, blocks, 256)
    keep.wait()
    got(("L", "f+", 2, 0), ("L", "f-", 2, 0))
    over((0, LEN), "A", 2, 0)
    got(("F", "z+", 0, 0), ("F", "z-", 0, 0))
    over_far(F_PART, "F", 0, 0)
    for d in (0, 4):
        got(("L", "y+", d, 0), ("L", "y-", d, 0))
        on_y(L_HALVES, "L", d, 0)
    for dy in (-1, 1):
        over_far(L_PART, "L", dy, 0)
    got(("L", "f+", 2, 1), ("L", "f-", 2, 1))
    over((0, LEN), "A", 2, 1)
    for shard in range(0, 2):
        left(win_ref, blocks, shard)
    got(("F", "z+", 0, 1), ("F", "z-", 0, 1))
    over_far(F_PART, "F", 0, 1)
    for dy in (-1, 1):
        got(("F", "z+", dy, 0), ("F", "z-", dy, 0))
        over_far(F_PART, "F", dy, 0)
        left(win_ref, blocks, 2 + (dy + 1) // 2)
    for d in (0, 4):
        got(("L", "y+", d, 1), ("L", "y-", d, 1))
        on_y(L_HALVES, "L", d, 1)
    for dy in (-1, 1):
        over_far(L_PART, "L", dy, 1)
    for n, (dy, dh) in enumerate(((-1, 1), (1, 1), (2, 0), (2, 1))):
        left(win_ref, blocks, 4 + n)
        got(("F", "z+", dy, dh), ("F", "z-", dy, dh))
        over_far(F_PART, "F", dy, dh)
    for dh in (0, 1):
        for d in (0, 4):
            got(("L", "f+", d, dh), ("L", "f-", d, dh))
        over_far(L_PART, "L", 2, dh)
    for name in copies:
        if name[1] in ("s", "t"):
            got(name)
    for copy in copies.values():
        copy.wait_send()

    loc = jnp.mod(columns_ref[...] - (b - 2) * ROWS, PANELS * ROWS)
    slot = g * SLOTS + lax.broadcasted_iota(jnp.int32, (SLOTS, ROWS), 0)
    live = slot < counts_ref[...]
    shard, within = loc // SHARD, loc % SHARD
    row = shard * LEN + HEAD + within // 2 * BS
    entry = (shard * 128 + within) * 2 + within % 2
    code_ref[0:SLOTS, :] = jnp.where(live, row, HEAD)
    code_ref[SLOTS:, :] = jnp.where(live, entry, SPAN * GROUP * 256)
    for n in range(SPAN * GROUP):
        near = win_ref[n // GROUP, n % GROUP, 0:HEAD, :].astype(F32)[0:1].astype(jnp.int32)
        table_ref[n : n + 1, :] = (near + n // GROUP * CB) * (2 * CB)
        if n // GROUP == 2:
            table_ref[n + 32 : n + 33, :] = near * 2
    table_ref[SPAN * GROUP : 48, :] = jnp.full((8, 128), TARGETS, jnp.int32)


COPIES = 86 - 8


def gathered(prolong, aggs, columns, counts, a):
    vmem, hbm = pl.BlockSpec(memory_space=pltpu.VMEM), pl.BlockSpec(memory_space=pltpu.HBM)
    return pl.pallas_call(
        gather_kernel,
        out_shape=(
            pltpu.VMEM((SPAN, GROUP, LEN, 2 * BS), BF16),
            pltpu.VMEM((ROWS, BS, 2 * BS), BF16),
            jax.ShapeDtypeStruct((2 * SLOTS, ROWS), jnp.int32),
            jax.ShapeDtypeStruct((56, 128), jnp.int32),
        ),
        in_specs=[hbm, vmem, vmem, vmem, hbm],
        out_specs=(vmem, vmem, vmem, vmem),
        scratch_shapes=[
            pltpu.VMEM((SHARD, BS, BS), BF16),
            pltpu.VMEM((LEN, 2 * BS), BF16),
            pltpu.VMEM((SLOTS, BS, BS, ROWS), BF16),
            pltpu.VMEM((BS * PITCH, 128), F32),
            pltpu.SemaphoreType.DMA((3,)),
            pltpu.SemaphoreType.DMA((COPIES,)),
            pltpu.SemaphoreType.DMA((COPIES,)),
        ],
        compiler_params=pltpu.CompilerParams(
            collective_id=0, has_side_effects=True, vmem_limit_bytes=20 * 2**20
        ),
        name="gather_window",
    )(
        pltpu.with_memory_space_constraint(prolong, pltpu.HBM),
        aggs,
        columns,
        counts,
        pltpu.with_memory_space_constraint(a, pltpu.HBM),
    )


def compute_kernel(code_ref, table_ref, win_ref, blocks, part_ref, acc):
    def clear(t, carry):
        acc[t] = jnp.zeros((BS, 2 * BS), F32)
        return carry

    lax.fori_loop(0, ACCS, clear, 0, unroll=8)

    for shard in range(GROUP):

        def right(j, carry, shard=shard):
            i = shard * SHARD + j
            none = jnp.zeros((BS, 2 * BS), BF16)
            column = table_ref[(48 + shard) * 128 + j]
            targets, picked = [], []
            for s in range(SLOTS):
                row = pl.multiple_of(code_ref[s, i], HEAD)
                entry = code_ref[SLOTS + s, i]
                picked.append(win_ref[pl.ds(row, BS), :])
                targets.append(table_ref[entry // 2] + column + entry % 2)
            stack = jnp.concatenate(
                [
                    jnp.concatenate([picked[0], none], axis=1),
                    jnp.concatenate([none, picked[1]], axis=1),
                ],
                axis=0,
            )
            r = jnp.dot(blocks[i], stack, preferred_element_type=F32)
            acc[targets[0]] += r[:, : 2 * BS]
            acc[targets[1]] += r[:, 2 * BS :]
            return carry

        lax.fori_loop(0, SHARD, right, 0, unroll=16)

    low = lax.broadcasted_iota(jnp.int32, (BS, 2 * BS), 1) < BS

    def fold(t, carry):
        one, two = acc[4 * t], acc[4 * t + 1]
        three, four = acc[4 * t + 2], acc[4 * t + 3]
        first = one + pltpu.roll(two, BS, 1)
        second = pltpu.roll(three, BS, 1) + four
        part_ref[t] = jnp.where(low, first, second)
        return carry

    lax.fori_loop(0, BLOCKS, fold, 0, unroll=4)


def computed(codes, table, win, blocks):
    smem = pl.BlockSpec(memory_space=pltpu.SMEM)
    vmem = pl.BlockSpec(memory_space=pltpu.VMEM)
    return pl.pallas_call(
        compute_kernel,
        out_shape=pltpu.VMEM((BLOCKS, BS, 2 * BS), F32),
        in_specs=[smem, smem, vmem, vmem],
        out_specs=vmem,
        scratch_shapes=[pltpu.VMEM((ACCS, BS, 2 * BS), F32)],
        compiler_params=pltpu.CompilerParams(vmem_limit_bytes=16 * 2**20),
        name="right_products",
    )(codes, table, win, blocks)


def reduce_kernel(part_ref, out_ref, landed, total, placed, send_sem, recv_sem, send2, recv2):
    b, g = lax.axis_index("blk"), lax.axis_index("grp")
    others = [(g + n) % GROUP for n in range(1, GROUP)]
    barrier = pltpu.get_barrier_semaphore()
    for other in others:
        pl.semaphore_signal(barrier, inc=1, device_id=(b, other), device_id_type=MESH)
    pl.semaphore_wait(barrier, GROUP - 1)
    first = []
    for n, other in enumerate(others):
        copy = pltpu.make_async_remote_copy(
            src_ref=part_ref.at[pl.ds(other * SHARE, SHARE)],
            dst_ref=landed.at[n],
            send_sem=send_sem.at[n],
            recv_sem=recv_sem.at[n],
            device_id=(b, other),
            device_id_type=MESH,
        )
        copy.start()
        first.append(copy)
    out_ref[...] = jnp.zeros(out_ref.shape, F32)
    total[...] = part_ref[pl.ds(g * SHARE, SHARE)]
    for n, copy in enumerate(first):
        copy.wait_recv()
        total[...] += landed[n]

    def owner(m):
        panel = (b + PANELS - 2 + m // 8) % PANELS
        return panel, panel // 2

    def hop(e, m, device):
        return pltpu.make_async_remote_copy(
            src_ref=total.at[e],
            dst_ref=placed.at[m],
            send_sem=send2.at[e],
            recv_sem=recv2.at[m],
            device_id=(b, device),
            device_id_type=MESH,
        )

    def keep(panel, m, block):
        row = (panel % 2) * CB + (m % 8) // 2
        column = (m % 2) * 2
        out_ref[row, column] = block[:, :BS]
        out_ref[row, column + 1] = block[:, BS:]

    for e in range(SHARE):
        m = g * SHARE + e
        panel, device = owner(m)

        @pl.when(device != g)
        def _(e=e, m=m, device=device):
            hop(e, m, device).start()

        @pl.when(device == g)
        def _(e=e, m=m, panel=panel):
            keep(panel, m, total[e])

    def arrive(m, carry):
        panel, device = owner(m)

        @pl.when(jnp.logical_and(device == g, m // SHARE != g))
        def _():
            hop(0, m, (g + 1) % GROUP).wait_recv()
            keep(panel, m, placed[m])

        return carry

    lax.fori_loop(0, BLOCKS, arrive, 0)
    for e in range(SHARE):
        m = g * SHARE + e
        panel, device = owner(m)

        @pl.when(device != g)
        def _(e=e, m=m, device=device):
            hop(e, m, device).wait_send()

    for copy in first:
        copy.wait_send()


def reduced(part):
    vmem = pl.BlockSpec(memory_space=pltpu.VMEM)
    return pl.pallas_call(
        reduce_kernel,
        out_shape=jax.ShapeDtypeStruct((GROUP, CB, BS, BS), F32),
        in_specs=[vmem],
        out_specs=vmem,
        scratch_shapes=[
            pltpu.VMEM((GROUP - 1, SHARE, BS, 2 * BS), F32),
            pltpu.VMEM((SHARE, BS, 2 * BS), F32),
            pltpu.VMEM((BLOCKS, BS, 2 * BS), F32),
            pltpu.SemaphoreType.DMA((GROUP - 1,)),
            pltpu.SemaphoreType.DMA((GROUP - 1,)),
            pltpu.SemaphoreType.DMA((SHARE,)),
            pltpu.SemaphoreType.DMA((BLOCKS,)),
        ],
        compiler_params=pltpu.CompilerParams(
            collective_id=1, has_side_effects=True, vmem_limit_bytes=12 * 2**20
        ),
        name="reduce_blocks",
    )(part)


def local(block_values, block_columns, row_counts, prolong_blocks, aggregates):
    win, blocks, codes, table = gathered(
        prolong_blocks,
        aggregates[None, :],
        block_columns.T,
        row_counts[None, :],
        jnp.transpose(block_values, (1, 2, 3, 0)),
    )
    win = win.reshape(-1, 2 * BS)
    return reduced(computed(codes, table.reshape(-1), win, blocks))


def solution(mesh):
    in_specs = (
        P("blk", "grp", None, None),
        P("blk", "grp"),
        P("blk"),
        P(("blk", "grp"), None, None),
        P(("blk", "grp")),
    )
    out_specs = P("grp", "blk", None, None)
    return jax.shard_map(local, mesh=mesh, in_specs=in_specs, out_specs=out_specs, check_vma=False)
```

```python
import functools

import jax
import jax.numpy as jnp
from jax import lax
from jax.experimental import pallas as pl
from jax.experimental.pallas import tpu as pltpu
from jax.sharding import PartitionSpec as P

MESH = pl.DeviceIdType.MESH
BF16, F32 = jnp.bfloat16, jnp.float32

BS = 64
CB = 4
ROWS = 384
SHARD = 48
PAIRS = SHARD // 2
PANELS = 16
GROUP = 8
SPAN = 5
HEAD = 16
LEN = HEAD + PAIRS * BS
CUT = HEAD + 14 * BS
F_PART, L_PART = (0, CUT), (CUT, LEN - CUT)
F_HALVES = ((0, 448), (448, CUT - 448))
L_HALVES = ((CUT, 320), (CUT + 320, 320))
SLOTS = 2
TARGETS = SPAN * CB * CB * 2
ACCS = TARGETS + 8
BLOCKS = TARGETS // 4
PITCH = 136


def turn(a_ref, turned, blocks, first):
    def over(r, carry):
        both = jnp.concatenate(
            [a_ref[s, r, :, first : first + 128] for s in range(SLOTS)], axis=0
        )
        start = pl.multiple_of(r * PITCH, 8)
        turned[pl.ds(start, 128), :] = both.T.astype(F32)
        return carry

    lax.fori_loop(0, BS, over, 0, unroll=16)

    def collect(i, carry):
        blocks[first + i] = turned[pl.ds(i, BS, stride=PITCH), :].astype(BF16)
        return carry

    lax.fori_loop(0, 128, collect, 0, unroll=16)


def left(win_ref, blocks, shard):
    def pair(j, carry):
        start = pl.multiple_of(HEAD + j * BS, HEAD)
        both = win_ref[2, shard, pl.ds(start, BS), :].T
        for half in range(2):
            i = shard * SHARD + 2 * j + half
            t = jnp.dot(
                both[half * BS : (half + 1) * BS, :], blocks[i], preferred_element_type=F32
            )
            blocks[i] = t.astype(BF16)
        return carry

    lax.fori_loop(0, PAIRS, pair, 0, unroll=12)


def gather_kernel(
    p_ref, agg_hbm, columns_hbm, counts_hbm, a_hbm,
    win_ref, blocks, code_ref, table_ref,
    raw, own, a_ref, turned, agg_ref, columns_ref, counts_ref,
    local_sem, send_sem, recv_sem,
):
    b, g = lax.axis_index("blk"), lax.axis_index("grp")
    core = b % 2
    y, h = g // 2, g % 2
    other = g + 1 - 2 * h
    z = (b // 2) % 4
    up_end = jnp.where(z == 3, 1, 0)
    down_end = jnp.where(z == 0, 1, 0)

    def on_k(step, end, dh):
        return (b + step + PANELS) % PANELS, g + dh * end * (1 - 2 * h)

    up_y, down_y = (b, (g + 2) % GROUP), (b, (g + GROUP - 2) % GROUP)
    across, sibling = (b, other), (b + 1 - 2 * core, g)

    load = pltpu.make_async_copy(p_ref, raw, local_sem.at[0])
    load.start()
    small = [
        pltpu.make_async_copy(source, target, local_sem.at[3 + n])
        for n, (source, target) in enumerate(
            ((agg_hbm, agg_ref), (columns_hbm, columns_ref), (counts_hbm, counts_ref))
        )
    ]
    for copy in small:
        copy.start()
    barrier = pltpu.get_barrier_semaphore()
    greeted = [up_y, down_y, across, sibling]
    for step in (2, PANELS - 2):
        greeted += [((b + step) % PANELS, column) for column in (g, other)]
    for device in greeted:
        pl.semaphore_signal(barrier, inc=1, device_id=device, device_id_type=MESH)
    small[0].wait()
    own[0:HEAD, :] = jnp.zeros((HEAD, 2 * BS), BF16)
    own[0:HEAD, 0:SHARD] = jnp.broadcast_to(
        (agg_ref[...] % CB).astype(F32).reshape(1, SHARD), (HEAD, SHARD)
    ).astype(BF16)
    load.wait()
    load_a = pltpu.make_async_copy(a_hbm, a_ref, local_sem.at[2])
    load_a.start()

    def pack(j, carry):
        row = pl.multiple_of(HEAD + j * BS, HEAD)
        own[pl.ds(row, BS), :] = jnp.concatenate([raw[2 * j], raw[2 * j + 1]], axis=-1)
        return carry

    lax.fori_loop(0, PAIRS, pack, 0, unroll=8)
    keep = pltpu.make_async_copy(own, win_ref.at[2, g], local_sem.at[1])
    keep.start()
    pl.semaphore_wait(barrier, len(greeted))

    copies = {}

    def at(d, dy, dh):
        return win_ref.at[d, ((y + dy) % 4) * 2 + (h + dh) % 2]

    def send(name, part, d, dy, dh, to_d, device, src=None):
        start, size = part
        piece = pl.ds(start, size)
        n = len(copies)
        source = own if src is not None else at(d, dy, dh)
        copies[name] = pltpu.make_async_remote_copy(
            src_ref=source.at[piece, :],
            dst_ref=at(to_d, dy, dh).at[piece, :],
            send_sem=send_sem.at[n],
            recv_sem=recv_sem.at[n],
            device_id=device,
            device_id_type=MESH,
        )
        copies[name].start()

    def got(*names):
        for name in names:
            copies[name].wait_recv()

    def to_y(part, tag, d, dh, src=None):
        send((tag, "y+", d, dh), part, d, 0, dh, d, up_y, src)
        send((tag, "y-", d, dh), part, d, 0, dh, d, down_y, src)

    def on_y(halves, tag, d, dh):
        send((tag, "f+", d, dh), halves[0], d, -1, dh, d, up_y)
        send((tag, "f-", d, dh), halves[1], d, 1, dh, d, down_y)

    def to_z(part, tag, dy, dh, src=None):
        for sign, step, end, to_d in (("z+", 2, up_end, 0), ("z-", -2, down_end, 4)):
            column = dh * (1 - end)
            send((tag, sign, dy, dh), part, 2, dy, column, to_d, on_k(step, end, dh), src)

    def over(part, tag, dy, dh, src=None):
        send((tag, "s", dy, dh), part, 2, dy, dh, 1 + 2 * core, sibling, src)

    def over_far(part, tag, dy, dh):
        send((tag, "t", dy, dh), part, 4 - 4 * core, dy, dh, 3 - 2 * core, sibling)

    send(("F", "x"), F_PART, 2, 0, 0, 2, across, own)
    to_y(F_PART, "F", 2, 0, own)
    to_z(F_PART, "F", 0, 0, own)
    send(("L", "x"), L_PART, 2, 0, 0, 2, across, own)
    to_z(L_PART, "L", 0, 0, own)
    to_y(L_PART, "L", 2, 0, own)
    over((0, LEN), "A", 0, 0, own)

    load_a.wait()
    turn(a_ref, turned, blocks, 0)
    got(("F", "x"))
    to_y(F_PART, "F", 2, 1)
    keep.wait()
    to_z(F_PART, "F", 0, 1)
    got(("F", "y+", 2, 0), ("F", "y-", 2, 0))
    on_y(F_HALVES, "F", 2, 0)
    for dy in (-1, 1):
        to_z(F_PART, "F", dy, 0)
    got(("L", "x"))
    to_z(L_PART, "L", 0, 1)
    to_y(L_PART, "L", 2, 1)
    over((0, LEN), "A", 0, 1)
    got(("L", "y+", 2, 0), ("L", "y-", 2, 0))
    on_y(L_HALVES, "L", 2, 0)
    for dy in (-1, 1):
        over((0, LEN), "A", dy, 0)
    got(("L", "z+", 0, 0), ("L", "z-", 0, 0))
    for d in (0, 4):
        to_y(L_PART, "L", d, 0)
    over_far(L_PART, "L", 0, 0)
    turn(a_ref, turned, blocks, 128)
    got(("F", "y+", 2, 1), ("F", "y-", 2, 1))
    on_y(F_HALVES, "F", 2, 1)
    for dy in (-1, 1):
        to_z(F_PART, "F", dy, 1)
    got(("F", "f+", 2, 0), ("F", "f-", 2, 0))
    to_z(F_PART, "F", 2, 0)
    got(("L", "z+", 0, 1), ("L", "z-", 0, 1))
    for d in (0, 4):
        to_y(L_PART, "L", d, 1)
    over_far(L_PART, "L", 0, 1)
    got(("F", "f+", 2, 1), ("F", "f-", 2, 1))
    to_z(F_PART, "F", 2, 1)
    got(("L", "y+", 2, 1), ("L", "y-", 2, 1))
    on_y(L_HALVES, "L", 2, 1)
    for dy in (-1, 1):
        over((0, LEN), "A", dy, 1)
    turn(a_ref, turned, blocks, 256)
    got(("L", "f+", 2, 0), ("L", "f-", 2, 0))
    over((0, LEN), "A", 2, 0)
    got(("F", "z+", 0, 0), ("F", "z-", 0, 0))
    over_far(F_PART, "F", 0, 0)
    for d in (0, 4):
        got(("L", "y+", d, 0), ("L", "y-", d, 0))
        on_y(L_HALVES, "L", d, 0)
    for dy in (-1, 1):
        over_far(L_PART, "L", dy, 0)
    got(("L", "f+", 2, 1), ("L", "f-", 2, 1))
    over((0, LEN), "A", 2, 1)
    for shard in range(0, 2):
        left(win_ref, blocks, shard)
    got(("F", "z+", 0, 1), ("F", "z-", 0, 1))
    over_far(F_PART, "F", 0, 1)
    for dy in (-1, 1):
        got(("F", "z+", dy, 0), ("F", "z-", dy, 0))
        over_far(F_PART, "F", dy, 0)
        left(win_ref, blocks, 2 + (dy + 1) // 2)
    for d in (0, 4):
        got(("L", "y+", d, 1), ("L", "y-", d, 1))
        on_y(L_HALVES, "L", d, 1)
    for dy in (-1, 1):
        over_far(L_PART, "L", dy, 1)
    for n, (dy, dh) in enumerate(((-1, 1), (1, 1), (2, 0), (2, 1))):
        left(win_ref, blocks, 4 + n)
        got(("F", "z+", dy, dh), ("F", "z-", dy, dh))
        over_far(F_PART, "F", dy, dh)
    for dh in (0, 1):
        for d in (0, 4):
            got(("L", "f+", d, dh), ("L", "f-", d, dh))
        over_far(L_PART, "L", 2, dh)
    for name in copies:
        if name[1] in ("s", "t"):
            got(name)
    for copy in copies.values():
        copy.wait_send()

    for copy in small[1:]:
        copy.wait()
    loc = jnp.mod(columns_ref[...] - (b - 2) * ROWS, PANELS * ROWS)
    slot = g * SLOTS + lax.broadcasted_iota(jnp.int32, (SLOTS, ROWS), 0)
    live = slot < counts_ref[...].reshape(1, ROWS)
    shard, within = loc // SHARD, loc % SHARD
    row = shard * LEN + HEAD + within // 2 * BS
    entry = (shard * 128 + within) * 2 + within % 2
    code_ref[0:SLOTS, :] = jnp.where(live, row, HEAD)
    code_ref[SLOTS:, :] = jnp.where(live, entry, SPAN * GROUP * 256)
    for n in range(SPAN * GROUP):
        near = win_ref[n // GROUP, n % GROUP, 0:HEAD, :].astype(F32)[0:1].astype(jnp.int32)
        table_ref[n : n + 1, :] = (near + n // GROUP * CB) * (2 * CB)
        if n // GROUP == 2:
            table_ref[n + 32 : n + 33, :] = near * 2
    table_ref[SPAN * GROUP : 48, :] = jnp.full((8, 128), TARGETS, jnp.int32)


COPIES = 86 - 8


def gathered(prolong, aggs, columns, counts, a):
    vmem, hbm = pl.BlockSpec(memory_space=pltpu.VMEM), pl.BlockSpec(memory_space=pltpu.HBM)
    return pl.pallas_call(
        gather_kernel,
        out_shape=(
            pltpu.VMEM((SPAN, GROUP, LEN, 2 * BS), BF16),
            pltpu.VMEM((ROWS, BS, 2 * BS), BF16),
            jax.ShapeDtypeStruct((2 * SLOTS, ROWS), jnp.int32),
            jax.ShapeDtypeStruct((56, 128), jnp.int32),
        ),
        in_specs=[hbm] * 5,
        out_specs=(vmem, vmem, vmem, vmem),
        scratch_shapes=[
            pltpu.VMEM((SHARD, BS, BS), BF16),
            pltpu.VMEM((LEN, 2 * BS), BF16),
            pltpu.VMEM((SLOTS, BS, BS, ROWS), BF16),
            pltpu.VMEM((BS * PITCH, 128), F32),
            pltpu.VMEM((SHARD,), jnp.int32),
            pltpu.VMEM((SLOTS, ROWS), jnp.int32),
            pltpu.VMEM((ROWS,), jnp.int32),
            pltpu.SemaphoreType.DMA((6,)),
            pltpu.SemaphoreType.DMA((COPIES,)),
            pltpu.SemaphoreType.DMA((COPIES,)),
        ],
        compiler_params=pltpu.CompilerParams(
            collective_id=0, has_side_effects=True, vmem_limit_bytes=20 * 2**20
        ),
        name="gather_window",
    )(*(pltpu.with_memory_space_constraint(x, pltpu.HBM) for x in (prolong, aggs, columns, counts, a)))


def compute_kernel(code_ref, table_ref, win_ref, blocks, part_ref, acc):
    def clear(t, carry):
        acc[t] = jnp.zeros((BS, 2 * BS), F32)
        return carry

    lax.fori_loop(0, ACCS, clear, 0, unroll=8)

    for shard in range(GROUP):

        def right(j, carry, shard=shard):
            i = shard * SHARD + j
            none = jnp.zeros((BS, 2 * BS), BF16)
            column = table_ref[(48 + shard) * 128 + j]
            targets, picked = [], []
            for s in range(SLOTS):
                row = pl.multiple_of(code_ref[s, i], HEAD)
                entry = code_ref[SLOTS + s, i]
                picked.append(win_ref[pl.ds(row, BS), :])
                targets.append(table_ref[entry // 2] + column + entry % 2)
            stack = jnp.concatenate(
                [
                    jnp.concatenate([picked[0], none], axis=1),
                    jnp.concatenate([none, picked[1]], axis=1),
                ],
                axis=0,
            )
            r = jnp.dot(blocks[i], stack, preferred_element_type=F32)
            acc[targets[0]] += r[:, : 2 * BS]
            acc[targets[1]] += r[:, 2 * BS :]
            return carry

        lax.fori_loop(0, SHARD, right, 0, unroll=16)

    low = lax.broadcasted_iota(jnp.int32, (BS, 2 * BS), 1) < BS

    def fold(t, carry):
        one, two = acc[4 * t], acc[4 * t + 1]
        three, four = acc[4 * t + 2], acc[4 * t + 3]
        first = one + pltpu.roll(two, BS, 1)
        second = pltpu.roll(three, BS, 1) + four
        part_ref[t % GROUP * SPAN + t // GROUP] = jnp.where(low, first, second)
        return carry

    lax.fori_loop(0, BLOCKS, fold, 0, unroll=4)


def computed(codes, table, win, blocks):
    smem = pl.BlockSpec(memory_space=pltpu.SMEM)
    vmem = pl.BlockSpec(memory_space=pltpu.VMEM)
    return pl.pallas_call(
        compute_kernel,
        out_shape=pltpu.VMEM((BLOCKS, BS, 2 * BS), F32),
        in_specs=[smem, smem, vmem, vmem],
        out_specs=vmem,
        scratch_shapes=[pltpu.VMEM((ACCS, BS, 2 * BS), F32)],
        compiler_params=pltpu.CompilerParams(vmem_limit_bytes=16 * 2**20),
        name="right_products",
    )(codes, table, win, blocks)


def reduce_kernel(part_ref, out_ref, landed, total, placed, send_sem, recv_sem, send2, recv2):
    b, g = lax.axis_index("blk"), lax.axis_index("grp")
    others = [(g + n) % GROUP for n in range(1, GROUP)]
    barrier = pltpu.get_barrier_semaphore()
    for other in others:
        pl.semaphore_signal(barrier, inc=1, device_id=(b, other), device_id_type=MESH)
    pl.semaphore_wait(barrier, GROUP - 1)
    first = []
    for n, other in enumerate(others):
        copy = pltpu.make_async_remote_copy(
            src_ref=part_ref.at[pl.ds(other * SPAN, SPAN)],
            dst_ref=landed.at[n],
            send_sem=send_sem.at[n],
            recv_sem=recv_sem.at[n],
            device_id=(b, other),
            device_id_type=MESH,
        )
        copy.start()
        first.append(copy)
    out_ref[...] = jnp.zeros(out_ref.shape, F32)
    total[...] = part_ref[pl.ds(g * SPAN, SPAN)]
    for n, copy in enumerate(first):
        copy.wait_recv()
        total[...] += landed[n]

    def hop(d):
        panel = (b + PANELS - 2 + d) % PANELS
        owner, side = panel // 2, panel % 2
        copy = pltpu.make_async_remote_copy(
            src_ref=total.at[d],
            dst_ref=placed.at[side, g],
            send_sem=send2.at[d],
            recv_sem=recv2.at[side],
            device_id=(b, owner),
            device_id_type=MESH,
        )
        return owner, side, copy

    for d in range(SPAN):
        owner, side, copy = hop(d)

        @pl.when(owner != g)
        def _(copy=copy):
            copy.start()

        @pl.when(owner == g)
        def _(d=d, side=side):
            placed[side, g] = total[d]

    for side in range(2):
        d = (2 * g + side + PANELS + 2 - b) % PANELS

        @pl.when(d < SPAN)
        def _(side=side):
            rest = placed.at[side, pl.ds(0, GROUP - 1)]
            pltpu.make_async_remote_copy(
                src_ref=rest,
                dst_ref=rest,
                send_sem=send2.at[0],
                recv_sem=recv2.at[side],
                device_id=(b, others[0]),
                device_id_type=MESH,
            ).wait_recv()
            for n in range(GROUP):
                block = placed[side, n]
                row, column = side * CB + n // 2, n % 2 * 2
                out_ref[row, column] = block[:, :BS]
                out_ref[row, column + 1] = block[:, BS:]

    for d in range(SPAN):
        owner, side, copy = hop(d)

        @pl.when(owner != g)
        def _(copy=copy):
            copy.wait_send()

    for copy in first:
        copy.wait_send()


def reduced(part):
    vmem = pl.BlockSpec(memory_space=pltpu.VMEM)
    return pl.pallas_call(
        reduce_kernel,
        out_shape=jax.ShapeDtypeStruct((GROUP, CB, BS, BS), F32),
        in_specs=[vmem],
        out_specs=vmem,
        scratch_shapes=[
            pltpu.VMEM((GROUP - 1, SPAN, BS, 2 * BS), F32),
            pltpu.VMEM((SPAN, BS, 2 * BS), F32),
            pltpu.VMEM((2, GROUP, BS, 2 * BS), F32),
            pltpu.SemaphoreType.DMA((GROUP - 1,)),
            pltpu.SemaphoreType.DMA((GROUP - 1,)),
            pltpu.SemaphoreType.DMA((SPAN,)),
            pltpu.SemaphoreType.DMA((2,)),
        ],
        compiler_params=pltpu.CompilerParams(
            collective_id=1, has_side_effects=True, vmem_limit_bytes=12 * 2**20
        ),
        name="reduce_blocks",
    )(part)


def local(block_values, block_columns, row_counts, prolong_blocks, aggregates):
    win, blocks, codes, table = gathered(
        prolong_blocks,
        aggregates,
        block_columns.T,
        row_counts,
        jnp.transpose(block_values, (1, 2, 3, 0)),
    )
    win = win.reshape(-1, 2 * BS)
    return reduced(computed(codes, table.reshape(-1), win, blocks))


def solution(mesh):
    in_specs = (
        P("blk", "grp", None, None),
        P("blk", "grp"),
        P("blk"),
        P(("blk", "grp"), None, None),
        P(("blk", "grp")),
    )
    out_specs = P("grp", "blk", None, None)
    return jax.shard_map(local, mesh=mesh, in_specs=in_specs, out_specs=out_specs, check_vma=False)
```

```python
import functools

import jax
import jax.numpy as jnp
from jax import lax
from jax.experimental import pallas as pl
from jax.experimental.pallas import tpu as pltpu
from jax.sharding import PartitionSpec as P

MESH = pl.DeviceIdType.MESH
BF16, F32 = jnp.bfloat16, jnp.float32

BS = 64
CB = 4
ROWS = 384
SHARD = 48
PAIRS = SHARD // 2
PANELS = 16
GROUP = 8
SPAN = 5
HEAD = 16
LEN = HEAD + PAIRS * BS
CUT = HEAD + 13 * BS
F_PART, L_PART = (0, CUT), (CUT, LEN - CUT)
F_HALVES = ((0, 416), (416, CUT - 416))
L_HALVES = ((CUT, 352), (CUT + 352, 352))
SLOTS = 2
TARGETS = SPAN * CB * CB * 2
ACCS = TARGETS + 8
BLOCKS = TARGETS // 4
PITCH = 136


def turn(a_ref, turned, blocks, first):
    def over(r, carry):
        both = jnp.concatenate(
            [a_ref[s, r, :, first : first + 128] for s in range(SLOTS)], axis=0
        )
        start = pl.multiple_of(r * PITCH, 8)
        turned[pl.ds(start, 128), :] = both.T.astype(F32)
        return carry

    lax.fori_loop(0, BS, over, 0, unroll=16)

    def collect(i, carry):
        blocks[first + i] = turned[pl.ds(i, BS, stride=PITCH), :].astype(BF16)
        return carry

    lax.fori_loop(0, 128, collect, 0, unroll=16)


def left(win_ref, blocks, shard):
    def pair(j, carry):
        start = pl.multiple_of(HEAD + j * BS, HEAD)
        both = win_ref[2, shard, pl.ds(start, BS), :].T
        for half in range(2):
            i = shard * SHARD + 2 * j + half
            t = jnp.dot(
                both[half * BS : (half + 1) * BS, :], blocks[i], preferred_element_type=F32
            )
            blocks[i] = t.astype(BF16)
        return carry

    lax.fori_loop(0, PAIRS, pair, 0, unroll=12)


def gather_kernel(
    p_ref, agg_hbm, columns_hbm, counts_hbm, a_hbm,
    win_ref, blocks, code_ref, table_ref,
    raw, own, a_ref, turned, agg_ref, columns_ref, counts_ref,
    local_sem, send_sem, recv_sem,
):
    b, g = lax.axis_index("blk"), lax.axis_index("grp")
    core = b % 2
    y, h = g // 2, g % 2
    other = g + 1 - 2 * h
    z = (b // 2) % 4
    up_end = jnp.where(z == 3, 1, 0)
    down_end = jnp.where(z == 0, 1, 0)

    def on_k(step, end, dh):
        return (b + step + PANELS) % PANELS, g + dh * end * (1 - 2 * h)

    up_y, down_y = (b, (g + 2) % GROUP), (b, (g + GROUP - 2) % GROUP)
    across, sibling = (b, other), (b + 1 - 2 * core, g)

    load = pltpu.make_async_copy(p_ref, raw, local_sem.at[0])
    load.start()
    small = [
        pltpu.make_async_copy(source, target, local_sem.at[3 + n])
        for n, (source, target) in enumerate(
            ((agg_hbm, agg_ref), (columns_hbm, columns_ref), (counts_hbm, counts_ref))
        )
    ]
    for copy in small:
        copy.start()
    barrier = pltpu.get_barrier_semaphore()
    greeted = [up_y, down_y, across, sibling]
    for step in (2, PANELS - 2):
        greeted += [((b + step) % PANELS, column) for column in (g, other)]
    for device in greeted:
        pl.semaphore_signal(barrier, inc=1, device_id=device, device_id_type=MESH)
    small[0].wait()
    own[0:HEAD, :] = jnp.zeros((HEAD, 2 * BS), BF16)
    own[0:HEAD, 0:SHARD] = jnp.broadcast_to(
        (agg_ref[...] % CB).astype(F32).reshape(1, SHARD), (HEAD, SHARD)
    ).astype(BF16)
    load.wait()
    load_a = pltpu.make_async_copy(a_hbm, a_ref, local_sem.at[2])
    load_a.start()

    def pack(j, carry):
        row = pl.multiple_of(HEAD + j * BS, HEAD)
        own[pl.ds(row, BS), :] = jnp.concatenate([raw[2 * j], raw[2 * j + 1]], axis=-1)
        return carry

    lax.fori_loop(0, PAIRS, pack, 0, unroll=8)
    keep = pltpu.make_async_copy(own, win_ref.at[2, g], local_sem.at[1])
    keep.start()
    pl.semaphore_wait(barrier, len(greeted))

    copies = {}

    def at(d, dy, dh):
        return win_ref.at[d, ((y + dy) % 4) * 2 + (h + dh) % 2]

    def send(name, part, d, dy, dh, to_d, device, src=None):
        start, size = part
        piece = pl.ds(start, size)
        n = len(copies)
        source = own if src is not None else at(d, dy, dh)
        copies[name] = pltpu.make_async_remote_copy(
            src_ref=source.at[piece, :],
            dst_ref=at(to_d, dy, dh).at[piece, :],
            send_sem=send_sem.at[n],
            recv_sem=recv_sem.at[n],
            device_id=device,
            device_id_type=MESH,
        )
        copies[name].start()

    def got(*names):
        for name in names:
            copies[name].wait_recv()

    def to_y(part, tag, d, dh, src=None):
        send((tag, "y+", d, dh), part, d, 0, dh, d, up_y, src)
        send((tag, "y-", d, dh), part, d, 0, dh, d, down_y, src)

    def on_y(halves, tag, d, dh):
        send((tag, "f+", d, dh), halves[0], d, -1, dh, d, up_y)
        send((tag, "f-", d, dh), halves[1], d, 1, dh, d, down_y)

    def to_z(part, tag, dy, dh, src=None):
        for sign, step, end, to_d in (("z+", 2, up_end, 0), ("z-", -2, down_end, 4)):
            column = dh * (1 - end)
            send((tag, sign, dy, dh), part, 2, dy, column, to_d, on_k(step, end, dh), src)

    def over(part, tag, dy, dh, src=None):
        send((tag, "s", dy, dh), part, 2, dy, dh, 1 + 2 * core, sibling, src)

    def over_far(part, tag, dy, dh):
        send((tag, "t", dy, dh), part, 4 - 4 * core, dy, dh, 3 - 2 * core, sibling)

    send(("F", "x"), F_PART, 2, 0, 0, 2, across, own)
    to_y(F_PART, "F", 2, 0, own)
    to_z(F_PART, "F", 0, 0, own)
    send(("L", "x"), L_PART, 2, 0, 0, 2, across, own)
    to_z(L_PART, "L", 0, 0, own)
    to_y(L_PART, "L", 2, 0, own)
    over((0, LEN), "A", 0, 0, own)

    load_a.wait()
    turn(a_ref, turned, blocks, 0)
    got(("F", "x"))
    to_y(F_PART, "F", 2, 1)
    keep.wait()
    to_z(F_PART, "F", 0, 1)
    got(("F", "y+", 2, 0), ("F", "y-", 2, 0))
    on_y(F_HALVES, "F", 2, 0)
    for dy in (-1, 1):
        to_z(F_PART, "F", dy, 0)
    got(("L", "x"))
    to_z(L_PART, "L", 0, 1)
    to_y(L_PART, "L", 2, 1)
    over((0, LEN), "A", 0, 1)
    got(("L", "y+", 2, 0), ("L", "y-", 2, 0))
    on_y(L_HALVES, "L", 2, 0)
    for dy in (-1, 1):
        over((0, LEN), "A", dy, 0)
    got(("L", "z+", 0, 0), ("L", "z-", 0, 0))
    for d in (0, 4):
        to_y(L_PART, "L", d, 0)
    over_far(L_PART, "L", 0, 0)
    turn(a_ref, turned, blocks, 128)
    got(("F", "y+", 2, 1), ("F", "y-", 2, 1))
    on_y(F_HALVES, "F", 2, 1)
    for dy in (-1, 1):
        to_z(F_PART, "F", dy, 1)
    got(("F", "f+", 2, 0), ("F", "f-", 2, 0))
    to_z(F_PART, "F", 2, 0)
    got(("L", "z+", 0, 1), ("L", "z-", 0, 1))
    for d in (0, 4):
        to_y(L_PART, "L", d, 1)
    over_far(L_PART, "L", 0, 1)
    got(("F", "f+", 2, 1), ("F", "f-", 2, 1))
    to_z(F_PART, "F", 2, 1)
    got(("L", "y+", 2, 1), ("L", "y-", 2, 1))
    on_y(L_HALVES, "L", 2, 1)
    for dy in (-1, 1):
        over((0, LEN), "A", dy, 1)
    turn(a_ref, turned, blocks, 256)
    got(("L", "f+", 2, 0), ("L", "f-", 2, 0))
    over((0, LEN), "A", 2, 0)
    got(("F", "z+", 0, 0), ("F", "z-", 0, 0))
    over_far(F_PART, "F", 0, 0)
    for d in (0, 4):
        got(("L", "y+", d, 0), ("L", "y-", d, 0))
        on_y(L_HALVES, "L", d, 0)
    for dy in (-1, 1):
        over_far(L_PART, "L", dy, 0)
    got(("L", "f+", 2, 1), ("L", "f-", 2, 1))
    over((0, LEN), "A", 2, 1)
    for shard in range(0, 2):
        left(win_ref, blocks, shard)
    got(("F", "z+", 0, 1), ("F", "z-", 0, 1))
    over_far(F_PART, "F", 0, 1)
    for dy in (-1, 1):
        got(("F", "z+", dy, 0), ("F", "z-", dy, 0))
        over_far(F_PART, "F", dy, 0)
        left(win_ref, blocks, 2 + (dy + 1) // 2)
    for d in (0, 4):
        got(("L", "y+", d, 1), ("L", "y-", d, 1))
        on_y(L_HALVES, "L", d, 1)
    for dy in (-1, 1):
        over_far(L_PART, "L", dy, 1)
    for n, (dy, dh) in enumerate(((-1, 1), (1, 1), (2, 0), (2, 1))):
        left(win_ref, blocks, 4 + n)
        got(("F", "z+", dy, dh), ("F", "z-", dy, dh))
        over_far(F_PART, "F", dy, dh)
    for dh in (0, 1):
        for d in (0, 4):
            got(("L", "f+", d, dh), ("L", "f-", d, dh))
        over_far(L_PART, "L", 2, dh)
    for name in copies:
        if name[1] in ("s", "t"):
            got(name)
    for copy in copies.values():
        copy.wait_send()

    for copy in small[1:]:
        copy.wait()
    loc = jnp.mod(columns_ref[...] - (b - 2) * ROWS, PANELS * ROWS)
    slot = g * SLOTS + lax.broadcasted_iota(jnp.int32, (SLOTS, ROWS), 0)
    live = slot < counts_ref[...].reshape(1, ROWS)
    shard, within = loc // SHARD, loc % SHARD
    row = shard * LEN + HEAD + within // 2 * BS
    entry = (shard * 128 + within) * 2 + within % 2
    code_ref[0:SLOTS, :] = jnp.where(live, row, HEAD)
    code_ref[SLOTS:, :] = jnp.where(live, entry, SPAN * GROUP * 256)
    for n in range(SPAN * GROUP):
        near = win_ref[n // GROUP, n % GROUP, 0:HEAD, :].astype(F32)[0:1].astype(jnp.int32)
        table_ref[n : n + 1, :] = (near + n // GROUP * CB) * (2 * CB)
        if n // GROUP == 2:
            table_ref[n + 32 : n + 33, :] = near * 2
    table_ref[SPAN * GROUP : 48, :] = jnp.full((8, 128), TARGETS, jnp.int32)


COPIES = 86 - 8


def gathered(prolong, aggs, columns, counts, a):
    vmem, hbm = pl.BlockSpec(memory_space=pltpu.VMEM), pl.BlockSpec(memory_space=pltpu.HBM)
    return pl.pallas_call(
        gather_kernel,
        out_shape=(
            pltpu.VMEM((SPAN, GROUP, LEN, 2 * BS), BF16),
            pltpu.VMEM((ROWS, BS, 2 * BS), BF16),
            jax.ShapeDtypeStruct((2 * SLOTS, ROWS), jnp.int32),
            jax.ShapeDtypeStruct((56, 128), jnp.int32),
        ),
        in_specs=[hbm] * 5,
        out_specs=(vmem, vmem, vmem, vmem),
        scratch_shapes=[
            pltpu.VMEM((SHARD, BS, BS), BF16),
            pltpu.VMEM((LEN, 2 * BS), BF16),
            pltpu.VMEM((SLOTS, BS, BS, ROWS), BF16),
            pltpu.VMEM((BS * PITCH, 128), F32),
            pltpu.VMEM((SHARD,), jnp.int32),
            pltpu.VMEM((SLOTS, ROWS), jnp.int32),
            pltpu.VMEM((ROWS,), jnp.int32),
            pltpu.SemaphoreType.DMA((6,)),
            pltpu.SemaphoreType.DMA((COPIES,)),
            pltpu.SemaphoreType.DMA((COPIES,)),
        ],
        compiler_params=pltpu.CompilerParams(
            collective_id=0, has_side_effects=True, vmem_limit_bytes=20 * 2**20
        ),
        name="gather_window",
    )(*(pltpu.with_memory_space_constraint(x, pltpu.HBM) for x in (prolong, aggs, columns, counts, a)))


def compute_kernel(code_ref, table_ref, win_ref, blocks, part_ref, short_ref, acc):
    def clear(t, carry):
        acc[t] = jnp.zeros((BS, 2 * BS), F32)
        return carry

    lax.fori_loop(0, ACCS, clear, 0, unroll=8)

    for shard in range(GROUP):

        def right(j, carry, shard=shard):
            i = shard * SHARD + j
            none = jnp.zeros((BS, 2 * BS), BF16)
            column = table_ref[(48 + shard) * 128 + j]
            targets, picked = [], []
            for s in range(SLOTS):
                row = pl.multiple_of(code_ref[s, i], HEAD)
                entry = code_ref[SLOTS + s, i]
                picked.append(win_ref[pl.ds(row, BS), :])
                targets.append(table_ref[entry // 2] + column + entry % 2)
            stack = jnp.concatenate(
                [
                    jnp.concatenate([picked[0], none], axis=1),
                    jnp.concatenate([none, picked[1]], axis=1),
                ],
                axis=0,
            )
            r = jnp.dot(blocks[i], stack, preferred_element_type=F32)
            acc[targets[0]] += r[:, : 2 * BS]
            acc[targets[1]] += r[:, 2 * BS :]
            return carry

        lax.fori_loop(0, SHARD, right, 0, unroll=SHARD)

    low = lax.broadcasted_iota(jnp.int32, (BS, 2 * BS), 1) < BS

    def fold(t, carry):
        one, two = acc[4 * t], acc[4 * t + 1]
        three, four = acc[4 * t + 2], acc[4 * t + 3]
        first = one + pltpu.roll(two, BS, 1)
        second = pltpu.roll(three, BS, 1) + four
        place = t % GROUP * SPAN + t // GROUP
        block = jnp.where(low, first, second)
        part_ref[place] = block
        short_ref[place] = block.astype(BF16)
        return carry

    lax.fori_loop(0, BLOCKS, fold, 0, unroll=4)


def computed(codes, table, win, blocks):
    smem = pl.BlockSpec(memory_space=pltpu.SMEM)
    vmem = pl.BlockSpec(memory_space=pltpu.VMEM)
    return pl.pallas_call(
        compute_kernel,
        out_shape=(
            pltpu.VMEM((BLOCKS, BS, 2 * BS), F32),
            pltpu.VMEM((BLOCKS, BS, 2 * BS), BF16),
        ),
        in_specs=[smem, smem, vmem, vmem],
        out_specs=(vmem, vmem),
        scratch_shapes=[pltpu.VMEM((ACCS, BS, 2 * BS), F32)],
        compiler_params=pltpu.CompilerParams(vmem_limit_bytes=16 * 2**20),
        name="right_products",
    )(codes, table, win, blocks)


def reduce_kernel(
    part_ref, short_ref, out_ref, landed, landed_short, total, placed,
    send_sem, recv_sem, send2, recv2,
):
    b, g = lax.axis_index("blk"), lax.axis_index("grp")
    others = [(g + n) % GROUP for n in range(1, GROUP)]
    barrier = pltpu.get_barrier_semaphore()
    for other in others:
        pl.semaphore_signal(barrier, inc=1, device_id=(b, other), device_id_type=MESH)
    pl.semaphore_wait(barrier, GROUP - 1)
    first = []
    for n, other in enumerate(others):
        source, target = (part_ref, landed) if n % 2 else (short_ref, landed_short)
        copy = pltpu.make_async_remote_copy(
            src_ref=source.at[pl.ds(other * SPAN, SPAN)],
            dst_ref=target.at[n // 2],
            send_sem=send_sem.at[n],
            recv_sem=recv_sem.at[n],
            device_id=(b, other),
            device_id_type=MESH,
        )
        copy.start()
        first.append(copy)
    out_ref[...] = jnp.zeros(out_ref.shape, F32)
    total[...] = part_ref[pl.ds(g * SPAN, SPAN)]
    for n, copy in enumerate(first):
        copy.wait_recv()
        total[...] += (landed if n % 2 else landed_short)[n // 2].astype(F32)

    def hop(d):
        panel = (b + PANELS - 2 + d) % PANELS
        owner, side = panel // 2, panel % 2
        copy = pltpu.make_async_remote_copy(
            src_ref=total.at[d],
            dst_ref=placed.at[side, g],
            send_sem=send2.at[d],
            recv_sem=recv2.at[side],
            device_id=(b, owner),
            device_id_type=MESH,
        )
        return owner, side, copy

    for d in range(SPAN):
        owner, side, copy = hop(d)

        @pl.when(owner != g)
        def _(copy=copy):
            copy.start()

        @pl.when(owner == g)
        def _(d=d, side=side):
            placed[side, g] = total[d]

    for side in range(2):
        d = (2 * g + side + PANELS + 2 - b) % PANELS

        @pl.when(d < SPAN)
        def _(side=side):
            rest = placed.at[side, pl.ds(0, GROUP - 1)]
            pltpu.make_async_remote_copy(
                src_ref=rest,
                dst_ref=rest,
                send_sem=send2.at[0],
                recv_sem=recv2.at[side],
                device_id=(b, others[0]),
                device_id_type=MESH,
            ).wait_recv()
            for n in range(GROUP):
                block = placed[side, n]
                row, column = side * CB + n // 2, n % 2 * 2
                out_ref[row, column] = block[:, :BS]
                out_ref[row, column + 1] = block[:, BS:]

    for d in range(SPAN):
        owner, side, copy = hop(d)

        @pl.when(owner != g)
        def _(copy=copy):
            copy.wait_send()

    for copy in first:
        copy.wait_send()


def reduced(part, short):
    vmem = pl.BlockSpec(memory_space=pltpu.VMEM)
    return pl.pallas_call(
        reduce_kernel,
        out_shape=jax.ShapeDtypeStruct((GROUP, CB, BS, BS), F32),
        in_specs=[vmem, vmem],
        out_specs=vmem,
        scratch_shapes=[
            pltpu.VMEM((GROUP // 2 - 1, SPAN, BS, 2 * BS), F32),
            pltpu.VMEM((GROUP // 2, SPAN, BS, 2 * BS), BF16),
            pltpu.VMEM((SPAN, BS, 2 * BS), F32),
            pltpu.VMEM((2, GROUP, BS, 2 * BS), F32),
            pltpu.SemaphoreType.DMA((GROUP - 1,)),
            pltpu.SemaphoreType.DMA((GROUP - 1,)),
            pltpu.SemaphoreType.DMA((SPAN,)),
            pltpu.SemaphoreType.DMA((2,)),
        ],
        compiler_params=pltpu.CompilerParams(
            collective_id=1, has_side_effects=True, vmem_limit_bytes=12 * 2**20
        ),
        name="reduce_blocks",
    )(part, short)


def local(block_values, block_columns, row_counts, prolong_blocks, aggregates):
    win, blocks, codes, table = gathered(
        prolong_blocks,
        aggregates,
        block_columns.T,
        row_counts,
        jnp.transpose(block_values, (1, 2, 3, 0)),
    )
    win = win.reshape(-1, 2 * BS)
    return reduced(*computed(codes, table.reshape(-1), win, blocks))


def solution(mesh):
    in_specs = (
        P("blk", "grp", None, None),
        P("blk", "grp"),
        P("blk"),
        P(("blk", "grp"), None, None),
        P(("blk", "grp")),
    )
    out_specs = P("grp", "blk", None, None)
    return jax.shard_map(local, mesh=mesh, in_specs=in_specs, out_specs=out_specs, check_vma=False)
```

```python
import functools

import jax
import jax.numpy as jnp
from jax import lax
from jax.experimental import pallas as pl
from jax.experimental.pallas import tpu as pltpu
from jax.sharding import PartitionSpec as P

MESH = pl.DeviceIdType.MESH
BF16, F32 = jnp.bfloat16, jnp.float32

BS = 64
CB = 4
ROWS = 384
SHARD = 48
PAIRS = SHARD // 2
PANELS = 16
GROUP = 8
SPAN = 5
HEAD = 16
LEN = HEAD + PAIRS * BS
CUT = HEAD + 13 * BS
F_PART, L_PART = (0, CUT), (CUT, LEN - CUT)
F_HALVES = ((0, 416), (416, CUT - 416))
L_HALVES = ((CUT, 352), (CUT + 352, 352))
SLOTS = 2
TARGETS = SPAN * CB * CB * 2
ACCS = TARGETS + 8
BLOCKS = TARGETS // 4
PITCH = 136


def turn(a_ref, turned, blocks, first):
    def over(r, carry):
        both = jnp.concatenate(
            [a_ref[s, r, :, first : first + 128] for s in range(SLOTS)], axis=0
        )
        start = pl.multiple_of(r * PITCH, 8)
        turned[pl.ds(start, 128), :] = both.T.astype(F32)
        return carry

    lax.fori_loop(0, BS, over, 0, unroll=16)

    def collect(i, carry):
        blocks[first + i] = turned[pl.ds(i, BS, stride=PITCH), :].astype(BF16)
        return carry

    lax.fori_loop(0, 128, collect, 0, unroll=16)


def left(win_ref, blocks, shard):
    def pair(j, carry):
        start = pl.multiple_of(HEAD + j * BS, HEAD)
        both = win_ref[2, shard, pl.ds(start, BS), :].T
        for half in range(2):
            i = shard * SHARD + 2 * j + half
            t = jnp.dot(
                both[half * BS : (half + 1) * BS, :], blocks[i], preferred_element_type=F32
            )
            blocks[i] = t.astype(BF16)
        return carry

    lax.fori_loop(0, PAIRS, pair, 0, unroll=12)


def gather_kernel(
    p_ref, agg_hbm, columns_hbm, counts_hbm, a_hbm,
    win_ref, blocks, code_ref, table_ref,
    raw, own, a_ref, turned, agg_ref, columns_ref, counts_ref,
    local_sem, send_sem, recv_sem,
):
    b, g = lax.axis_index("blk"), lax.axis_index("grp")
    core = b % 2
    y, h = g // 2, g % 2
    other = g + 1 - 2 * h
    z = (b // 2) % 4
    up_end = jnp.where(z == 3, 1, 0)
    down_end = jnp.where(z == 0, 1, 0)

    def on_k(step, end, dh):
        return (b + step + PANELS) % PANELS, g + dh * end * (1 - 2 * h)

    up_y, down_y = (b, (g + 2) % GROUP), (b, (g + GROUP - 2) % GROUP)
    across, sibling = (b, other), (b + 1 - 2 * core, g)

    load = pltpu.make_async_copy(p_ref, raw, local_sem.at[0])
    load.start()
    small = [
        pltpu.make_async_copy(source, target, local_sem.at[3 + n])
        for n, (source, target) in enumerate(
            ((agg_hbm, agg_ref), (columns_hbm, columns_ref), (counts_hbm, counts_ref))
        )
    ]
    for copy in small:
        copy.start()
    barrier = pltpu.get_barrier_semaphore()
    greeted = [up_y, down_y, across, sibling]
    for step in (2, PANELS - 2):
        greeted += [((b + step) % PANELS, column) for column in (g, other)]
    for device in greeted:
        pl.semaphore_signal(barrier, inc=1, device_id=device, device_id_type=MESH)
    small[0].wait()
    own[0:HEAD, :] = jnp.zeros((HEAD, 2 * BS), BF16)
    own[0:HEAD, 0:SHARD] = jnp.broadcast_to(
        (agg_ref[...] % CB).astype(F32).reshape(1, SHARD), (HEAD, SHARD)
    ).astype(BF16)
    load.wait()
    load_a = pltpu.make_async_copy(a_hbm, a_ref, local_sem.at[2])
    load_a.start()

    def pack(j, carry):
        row = pl.multiple_of(HEAD + j * BS, HEAD)
        own[pl.ds(row, BS), :] = jnp.concatenate([raw[2 * j], raw[2 * j + 1]], axis=-1)
        return carry

    lax.fori_loop(0, PAIRS, pack, 0, unroll=8)
    keep = pltpu.make_async_copy(own, win_ref.at[2, g], local_sem.at[1])
    keep.start()
    pl.semaphore_wait(barrier, len(greeted))

    copies = {}

    def at(d, dy, dh):
        return win_ref.at[d, ((y + dy) % 4) * 2 + (h + dh) % 2]

    def send(name, part, d, dy, dh, to_d, device, src=None):
        start, size = part
        piece = pl.ds(start, size)
        n = len(copies)
        source = own if src is not None else at(d, dy, dh)
        copies[name] = pltpu.make_async_remote_copy(
            src_ref=source.at[piece, :],
            dst_ref=at(to_d, dy, dh).at[piece, :],
            send_sem=send_sem.at[n],
            recv_sem=recv_sem.at[n],
            device_id=device,
            device_id_type=MESH,
        )
        copies[name].start()

    def got(*names):
        for name in names:
            copies[name].wait_recv()

    def to_y(part, tag, d, dh, src=None):
        send((tag, "y+", d, dh), part, d, 0, dh, d, up_y, src)
        send((tag, "y-", d, dh), part, d, 0, dh, d, down_y, src)

    def on_y(halves, tag, d, dh):
        send((tag, "f+", d, dh), halves[0], d, -1, dh, d, up_y)
        send((tag, "f-", d, dh), halves[1], d, 1, dh, d, down_y)

    def to_z(part, tag, dy, dh, src=None):
        for sign, step, end, to_d in (("z+", 2, up_end, 0), ("z-", -2, down_end, 4)):
            column = dh * (1 - end)
            send((tag, sign, dy, dh), part, 2, dy, column, to_d, on_k(step, end, dh), src)

    def over(part, tag, dy, dh, src=None):
        send((tag, "s", dy, dh), part, 2, dy, dh, 1 + 2 * core, sibling, src)

    def over_far(part, tag, dy, dh):
        send((tag, "t", dy, dh), part, 4 - 4 * core, dy, dh, 3 - 2 * core, sibling)

    send(("F", "x"), F_PART, 2, 0, 0, 2, across, own)
    to_y(F_PART, "F", 2, 0, own)
    to_z(F_PART, "F", 0, 0, own)
    send(("L", "x"), L_PART, 2, 0, 0, 2, across, own)
    to_z(L_PART, "L", 0, 0, own)
    to_y(L_PART, "L", 2, 0, own)
    over((0, LEN), "A", 0, 0, own)

    for copy in small[1:]:
        copy.wait()
    loc = jnp.mod(columns_ref[...] - (b - 2) * ROWS, PANELS * ROWS)
    slot = g * SLOTS + lax.broadcasted_iota(jnp.int32, (SLOTS, ROWS), 0)
    live = slot < counts_ref[...].reshape(1, ROWS)
    shard, within = loc // SHARD, loc % SHARD
    row = shard * LEN + HEAD + within // 2 * BS
    entry = (shard * 128 + within) * 2 + within % 2
    code_ref[0:SLOTS, :] = jnp.where(live, row, HEAD)
    code_ref[SLOTS:, :] = jnp.where(live, entry, SPAN * GROUP * 256)
    load_a.wait()
    turn(a_ref, turned, blocks, 0)
    got(("F", "x"))
    to_y(F_PART, "F", 2, 1)
    keep.wait()
    to_z(F_PART, "F", 0, 1)
    got(("F", "y+", 2, 0), ("F", "y-", 2, 0))
    on_y(F_HALVES, "F", 2, 0)
    for dy in (-1, 1):
        to_z(F_PART, "F", dy, 0)
    got(("L", "x"))
    to_z(L_PART, "L", 0, 1)
    to_y(L_PART, "L", 2, 1)
    over((0, LEN), "A", 0, 1)
    got(("L", "y+", 2, 0), ("L", "y-", 2, 0))
    on_y(L_HALVES, "L", 2, 0)
    for dy in (-1, 1):
        over((0, LEN), "A", dy, 0)
    got(("L", "z+", 0, 0), ("L", "z-", 0, 0))
    for d in (0, 4):
        to_y(L_PART, "L", d, 0)
    over_far(L_PART, "L", 0, 0)
    turn(a_ref, turned, blocks, 128)
    got(("F", "y+", 2, 1), ("F", "y-", 2, 1))
    on_y(F_HALVES, "F", 2, 1)
    for dy in (-1, 1):
        to_z(F_PART, "F", dy, 1)
    got(("F", "f+", 2, 0), ("F", "f-", 2, 0))
    to_z(F_PART, "F", 2, 0)
    got(("L", "z+", 0, 1), ("L", "z-", 0, 1))
    for d in (0, 4):
        to_y(L_PART, "L", d, 1)
    over_far(L_PART, "L", 0, 1)
    got(("F", "f+", 2, 1), ("F", "f-", 2, 1))
    to_z(F_PART, "F", 2, 1)
    got(("L", "y+", 2, 1), ("L", "y-", 2, 1))
    on_y(L_HALVES, "L", 2, 1)
    for dy in (-1, 1):
        over((0, LEN), "A", dy, 1)
    turn(a_ref, turned, blocks, 256)
    got(("L", "f+", 2, 0), ("L", "f-", 2, 0))
    over((0, LEN), "A", 2, 0)
    got(("F", "z+", 0, 0), ("F", "z-", 0, 0))
    over_far(F_PART, "F", 0, 0)
    for d in (0, 4):
        got(("L", "y+", d, 0), ("L", "y-", d, 0))
        on_y(L_HALVES, "L", d, 0)
    for dy in (-1, 1):
        over_far(L_PART, "L", dy, 0)
    got(("L", "f+", 2, 1), ("L", "f-", 2, 1))
    over((0, LEN), "A", 2, 1)
    for shard in range(0, 2):
        left(win_ref, blocks, shard)
    got(("F", "z+", 0, 1), ("F", "z-", 0, 1))
    over_far(F_PART, "F", 0, 1)
    for dy in (-1, 1):
        got(("F", "z+", dy, 0), ("F", "z-", dy, 0))
        over_far(F_PART, "F", dy, 0)
        left(win_ref, blocks, 2 + (dy + 1) // 2)
    for d in (0, 4):
        got(("L", "y+", d, 1), ("L", "y-", d, 1))
        on_y(L_HALVES, "L", d, 1)
    for dy in (-1, 1):
        over_far(L_PART, "L", dy, 1)
    for n, (dy, dh) in enumerate(((-1, 1), (1, 1), (2, 0), (2, 1))):
        left(win_ref, blocks, 4 + n)
        got(("F", "z+", dy, dh), ("F", "z-", dy, dh))
        over_far(F_PART, "F", dy, dh)
    for dh in (0, 1):
        for d in (0, 4):
            got(("L", "f+", d, dh), ("L", "f-", d, dh))
        over_far(L_PART, "L", 2, dh)
    for name in copies:
        if name[1] in ("s", "t"):
            got(name)
    for copy in copies.values():
        copy.wait_send()

    for n in range(SPAN * GROUP):
        near = win_ref[n // GROUP, n % GROUP, 0:HEAD, :].astype(F32)[0:1].astype(jnp.int32)
        table_ref[n : n + 1, :] = (near + n // GROUP * CB) * (2 * CB)
        if n // GROUP == 2:
            table_ref[n + 32 : n + 33, :] = near * 2
    table_ref[SPAN * GROUP : 48, :] = jnp.full((8, 128), TARGETS, jnp.int32)


COPIES = 86 - 8


def gathered(prolong, aggs, columns, counts, a):
    vmem, hbm = pl.BlockSpec(memory_space=pltpu.VMEM), pl.BlockSpec(memory_space=pltpu.HBM)
    return pl.pallas_call(
        gather_kernel,
        out_shape=(
            pltpu.VMEM((SPAN, GROUP, LEN, 2 * BS), BF16),
            pltpu.VMEM((ROWS, BS, 2 * BS), BF16),
            jax.ShapeDtypeStruct((2 * SLOTS, ROWS), jnp.int32),
            jax.ShapeDtypeStruct((56, 128), jnp.int32),
        ),
        in_specs=[hbm] * 5,
        out_specs=(vmem, vmem, vmem, vmem),
        scratch_shapes=[
            pltpu.VMEM((SHARD, BS, BS), BF16),
            pltpu.VMEM((LEN, 2 * BS), BF16),
            pltpu.VMEM((SLOTS, BS, BS, ROWS), BF16),
            pltpu.VMEM((BS * PITCH, 128), F32),
            pltpu.VMEM((SHARD,), jnp.int32),
            pltpu.VMEM((SLOTS, ROWS), jnp.int32),
            pltpu.VMEM((ROWS,), jnp.int32),
            pltpu.SemaphoreType.DMA((6,)),
            pltpu.SemaphoreType.DMA((COPIES,)),
            pltpu.SemaphoreType.DMA((COPIES,)),
        ],
        compiler_params=pltpu.CompilerParams(
            collective_id=0, has_side_effects=True, vmem_limit_bytes=20 * 2**20
        ),
        name="gather_window",
    )(*(pltpu.with_memory_space_constraint(x, pltpu.HBM) for x in (prolong, aggs, columns, counts, a)))


def compute_kernel(code_ref, table_ref, win_ref, blocks, part_ref, short_ref, acc):
    def clear(t, carry):
        acc[t] = jnp.zeros((BS, 2 * BS), F32)
        return carry

    lax.fori_loop(0, ACCS, clear, 0, unroll=8)

    for shard in range(GROUP):

        def right(j, carry, shard=shard):
            i = shard * SHARD + j
            none = jnp.zeros((BS, 2 * BS), BF16)
            column = table_ref[(48 + shard) * 128 + j]
            targets, picked = [], []
            for s in range(SLOTS):
                row = pl.multiple_of(code_ref[s, i], HEAD)
                entry = code_ref[SLOTS + s, i]
                picked.append(win_ref[pl.ds(row, BS), :])
                targets.append(table_ref[entry // 2] + column + entry % 2)
            stack = jnp.concatenate(
                [
                    jnp.concatenate([picked[0], none], axis=1),
                    jnp.concatenate([none, picked[1]], axis=1),
                ],
                axis=0,
            )
            r = jnp.dot(blocks[i], stack, preferred_element_type=F32)
            acc[targets[0]] += r[:, : 2 * BS]
            acc[targets[1]] += r[:, 2 * BS :]
            return carry

        lax.fori_loop(0, SHARD, right, 0, unroll=SHARD)

    low = lax.broadcasted_iota(jnp.int32, (BS, 2 * BS), 1) < BS

    def fold(t, carry):
        one, two = acc[4 * t], acc[4 * t + 1]
        three, four = acc[4 * t + 2], acc[4 * t + 3]
        first = one + pltpu.roll(two, BS, 1)
        second = pltpu.roll(three, BS, 1) + four
        panel, row, columns = t // GROUP, t % GROUP // 2, t % 2
        block = jnp.where(low, first, second)
        part_ref[columns, panel, row] = block
        short_ref[columns, panel, row] = block.astype(BF16)
        return carry

    lax.fori_loop(0, BLOCKS, fold, 0, unroll=4)


def computed(codes, table, win, blocks):
    smem = pl.BlockSpec(memory_space=pltpu.SMEM)
    vmem = pl.BlockSpec(memory_space=pltpu.VMEM)
    return pl.pallas_call(
        compute_kernel,
        out_shape=(
            pltpu.VMEM((2, SPAN, CB, BS, 2 * BS), F32),
            pltpu.VMEM((2, SPAN, CB, BS, 2 * BS), BF16),
        ),
        in_specs=[smem, smem, vmem, vmem],
        out_specs=(vmem, vmem),
        scratch_shapes=[pltpu.VMEM((ACCS, BS, 2 * BS), F32)],
        compiler_params=pltpu.CompilerParams(vmem_limit_bytes=16 * 2**20),
        name="right_products",
    )(codes, table, win, blocks)


def reduce_kernel(
    part_ref, short_ref, out_ref, crossed, sums, landed, total, placed,
    x_send, x_recv, y_send, y_recv, hop_send, hop_recv,
):
    b, g = lax.axis_index("blk"), lax.axis_index("grp")
    y, h = g // 2, g % 2
    mate = 1 - h
    others = [(g + n) % GROUP for n in range(1, GROUP)]
    barrier = pltpu.get_barrier_semaphore()
    for other in others:
        pl.semaphore_signal(barrier, inc=1, device_id=(b, other), device_id_type=MESH)
    pl.semaphore_wait(barrier, GROUP - 1)

    across = [
        pltpu.make_async_remote_copy(
            src_ref=short_ref.at[mate, d],
            dst_ref=crossed.at[d],
            send_sem=x_send.at[d],
            recv_sem=x_recv.at[d],
            device_id=(b, 2 * y + mate),
            device_id_type=MESH,
        )
        for d in range(SPAN)
    ]
    for copy in across:
        copy.start()
    out_ref[...] = jnp.zeros(out_ref.shape, F32)

    def along(d):
        return [
            pltpu.make_async_remote_copy(
                src_ref=sums.at[d, (y + n) % CB],
                dst_ref=landed.at[d, n - 1],
                send_sem=y_send.at[d, n - 1],
                recv_sem=y_recv.at[d, n - 1],
                device_id=(b, (g + 2 * n) % GROUP),
                device_id_type=MESH,
            )
            for n in range(1, CB)
        ]

    def hop(d):
        panel = (b + PANELS - 2 + d) % PANELS
        owner, side = panel // 2, panel % 2
        copy = pltpu.make_async_remote_copy(
            src_ref=total.at[d],
            dst_ref=placed.at[side, g],
            send_sem=hop_send.at[d],
            recv_sem=hop_recv.at[side],
            device_id=(b, owner),
            device_id_type=MESH,
        )
        return owner, side, copy

    rows = [along(d) for d in range(SPAN)]
    for step in range(SPAN + 1):
        if step < SPAN:
            across[step].wait_recv()
            sums[step] = part_ref[h, step] + crossed[step].astype(F32)
            for copy in rows[step]:
                copy.start()
        if step > 0:
            d = step - 1
            block = sums[d, y]
            for n, copy in enumerate(rows[d]):
                copy.wait_recv()
                block += landed[d, n]
            owner, side, copy = hop(d)
            total[d] = block

            @pl.when(owner != g)
            def _(copy=copy):
                copy.start()

            @pl.when(owner == g)
            def _(d=d, side=side):
                placed[side, g] = total[d]

    for side in range(2):
        d = (2 * g + side + PANELS + 2 - b) % PANELS

        @pl.when(d < SPAN)
        def _(side=side):
            rest = placed.at[side, pl.ds(0, GROUP - 1)]
            pltpu.make_async_remote_copy(
                src_ref=rest,
                dst_ref=rest,
                send_sem=hop_send.at[0],
                recv_sem=hop_recv.at[side],
                device_id=(b, others[0]),
                device_id_type=MESH,
            ).wait_recv()
            for n in range(GROUP):
                block = placed[side, n]
                row, column = side * CB + n // 2, n % 2 * 2
                out_ref[row, column] = block[:, :BS]
                out_ref[row, column + 1] = block[:, BS:]

    for d in range(SPAN):
        owner, side, copy = hop(d)

        @pl.when(owner != g)
        def _(copy=copy):
            copy.wait_send()

        for copy in [across[d]] + rows[d]:
            copy.wait_send()


def reduced(part, short):
    vmem = pl.BlockSpec(memory_space=pltpu.VMEM)
    block = (BS, 2 * BS)
    dma = pltpu.SemaphoreType.DMA
    return pl.pallas_call(
        reduce_kernel,
        out_shape=jax.ShapeDtypeStruct((GROUP, CB, BS, BS), F32),
        in_specs=[vmem, vmem],
        out_specs=vmem,
        scratch_shapes=[
            pltpu.VMEM((SPAN, CB, *block), BF16),
            pltpu.VMEM((SPAN, CB, *block), F32),
            pltpu.VMEM((SPAN, CB - 1, *block), F32),
            pltpu.VMEM((SPAN, *block), F32),
            pltpu.VMEM((2, GROUP, *block), F32),
            dma((SPAN,)),
            dma((SPAN,)),
            dma((SPAN, CB - 1)),
            dma((SPAN, CB - 1)),
            dma((SPAN,)),
            dma((2,)),
        ],
        compiler_params=pltpu.CompilerParams(
            collective_id=1, has_side_effects=True, vmem_limit_bytes=12 * 2**20
        ),
        name="reduce_blocks",
    )(part, short)


def local(block_values, block_columns, row_counts, prolong_blocks, aggregates):
    win, blocks, codes, table = gathered(
        prolong_blocks,
        aggregates,
        block_columns.T,
        row_counts,
        jnp.transpose(block_values, (1, 2, 3, 0)),
    )
    win = win.reshape(-1, 2 * BS)
    return reduced(*computed(codes, table.reshape(-1), win, blocks))


def solution(mesh):
    in_specs = (
        P("blk", "grp", None, None),
        P("blk", "grp"),
        P("blk"),
        P(("blk", "grp"), None, None),
        P(("blk", "grp")),
    )
    out_specs = P("grp", "blk", None, None)
    return jax.shard_map(local, mesh=mesh, in_specs=in_specs, out_specs=out_specs, check_vma=False)
```

```python
import functools

import jax
import jax.numpy as jnp
from jax import lax
from jax.experimental import pallas as pl
from jax.experimental.pallas import tpu as pltpu
from jax.sharding import PartitionSpec as P

MESH = pl.DeviceIdType.MESH
BF16, F32 = jnp.bfloat16, jnp.float32

BS = 64
CB = 4
ROWS = 384
SHARD = 48
PAIRS = SHARD // 2
PANELS = 16
GROUP = 8
SPAN = 5
HEAD = 16
LEN = HEAD + PAIRS * BS
CUT = HEAD + 13 * BS
F_PART, L_PART = (0, CUT), (CUT, LEN - CUT)
F_HALVES = ((0, 416), (416, CUT - 416))
L_HALVES = ((CUT, 352), (CUT + 352, 352))
SLOTS = 2
TARGETS = SPAN * CB * CB * 2
ACCS = TARGETS + 8
BLOCKS = TARGETS // 4
PITCH = 136


def turn(a_ref, turned, blocks, first):
    def over(r, carry):
        both = jnp.concatenate(
            [a_ref[s, r, :, first : first + 128] for s in range(SLOTS)], axis=0
        )
        start = pl.multiple_of(r * PITCH, 8)
        turned[pl.ds(start, 128), :] = both.T.astype(F32)
        return carry

    lax.fori_loop(0, BS, over, 0, unroll=16)

    def collect(i, carry):
        blocks[first + i] = turned[pl.ds(i, BS, stride=PITCH), :].astype(BF16)
        return carry

    lax.fori_loop(0, 128, collect, 0, unroll=16)


def left(win_ref, blocks, shard):
    def pair(j, carry):
        start = pl.multiple_of(HEAD + j * BS, HEAD)
        both = win_ref[2, shard, pl.ds(start, BS), :].T
        for half in range(2):
            i = shard * SHARD + 2 * j + half
            t = jnp.dot(
                both[half * BS : (half + 1) * BS, :], blocks[i], preferred_element_type=F32
            )
            blocks[i] = t.astype(BF16)
        return carry

    lax.fori_loop(0, PAIRS, pair, 0, unroll=12)


def gather_kernel(
    p_ref, agg_hbm, columns_hbm, counts_hbm, a_hbm,
    win_ref, blocks, code_ref, table_ref,
    raw, own, a_ref, turned, agg_ref, columns_ref, counts_ref,
    local_sem, send_sem, recv_sem,
):
    b, g = lax.axis_index("blk"), lax.axis_index("grp")
    core = b % 2
    y, h = g // 2, g % 2
    other = g + 1 - 2 * h
    z = (b // 2) % 4
    up_end = jnp.where(z == 3, 1, 0)
    down_end = jnp.where(z == 0, 1, 0)

    def on_k(step, end, dh):
        return (b + step + PANELS) % PANELS, g + dh * end * (1 - 2 * h)

    up_y, down_y = (b, (g + 2) % GROUP), (b, (g + GROUP - 2) % GROUP)
    across, sibling = (b, other), (b + 1 - 2 * core, g)

    load = pltpu.make_async_copy(p_ref, raw, local_sem.at[0])
    load.start()
    small = [
        pltpu.make_async_copy(source, target, local_sem.at[3 + n])
        for n, (source, target) in enumerate(
            ((agg_hbm, agg_ref), (columns_hbm, columns_ref), (counts_hbm, counts_ref))
        )
    ]
    for copy in small:
        copy.start()
    barrier = pltpu.get_barrier_semaphore()
    greeted = [up_y, down_y, across, sibling]
    for step in (2, PANELS - 2):
        greeted += [((b + step) % PANELS, column) for column in (g, other)]
    for device in greeted:
        pl.semaphore_signal(barrier, inc=1, device_id=device, device_id_type=MESH)
    small[0].wait()
    own[0:HEAD, :] = jnp.zeros((HEAD, 2 * BS), BF16)
    own[0:HEAD, 0:SHARD] = jnp.broadcast_to(
        (agg_ref[...] % CB).astype(F32).reshape(1, SHARD), (HEAD, SHARD)
    ).astype(BF16)
    load.wait()
    load_a = pltpu.make_async_copy(a_hbm, a_ref, local_sem.at[2])
    load_a.start()

    def pack(j, carry):
        row = pl.multiple_of(HEAD + j * BS, HEAD)
        own[pl.ds(row, BS), :] = jnp.concatenate([raw[2 * j], raw[2 * j + 1]], axis=-1)
        return carry

    lax.fori_loop(0, PAIRS, pack, 0, unroll=8)
    keep = pltpu.make_async_copy(own, win_ref.at[2, g], local_sem.at[1])
    keep.start()
    pl.semaphore_wait(barrier, len(greeted))

    copies, arrived, settled = {}, [], set()

    def at(d, dy, dh):
        return win_ref.at[d, ((y + dy) % 4) * 2 + (h + dh) % 2]

    def send(name, part, d, dy, dh, to_d, device, src=None):
        start, size = part
        piece = pl.ds(start, size)
        n = len(copies)
        source = own if src is not None else at(d, dy, dh)
        copies[name] = pltpu.make_async_remote_copy(
            src_ref=source.at[piece, :],
            dst_ref=at(to_d, dy, dh).at[piece, :],
            send_sem=send_sem.at[n],
            recv_sem=recv_sem.at[n],
            device_id=device,
            device_id_type=MESH,
        )
        copies[name].start()

    def got(*names):
        for name in names:
            copies[name].wait_recv()
            arrived.append(name)

    def settle():
        for name in arrived:
            if name not in settled:
                settled.add(name)
                copies[name].wait_send()

    def to_y(part, tag, d, dh, src=None):
        send((tag, "y+", d, dh), part, d, 0, dh, d, up_y, src)
        send((tag, "y-", d, dh), part, d, 0, dh, d, down_y, src)

    def on_y(halves, tag, d, dh):
        send((tag, "f+", d, dh), halves[0], d, -1, dh, d, up_y)
        send((tag, "f-", d, dh), halves[1], d, 1, dh, d, down_y)

    def to_z(part, tag, dy, dh, src=None):
        for sign, step, end, to_d in (("z+", 2, up_end, 0), ("z-", -2, down_end, 4)):
            column = dh * (1 - end)
            send((tag, sign, dy, dh), part, 2, dy, column, to_d, on_k(step, end, dh), src)

    def over(part, tag, dy, dh, src=None):
        send((tag, "s", dy, dh), part, 2, dy, dh, 1 + 2 * core, sibling, src)

    def over_far(part, tag, dy, dh):
        send((tag, "t", dy, dh), part, 4 - 4 * core, dy, dh, 3 - 2 * core, sibling)

    send(("F", "x"), F_PART, 2, 0, 0, 2, across, own)
    to_y(F_PART, "F", 2, 0, own)
    to_z(F_PART, "F", 0, 0, own)
    send(("L", "x"), L_PART, 2, 0, 0, 2, across, own)
    to_z(L_PART, "L", 0, 0, own)
    to_y(L_PART, "L", 2, 0, own)
    over((0, LEN), "A", 0, 0, own)

    for copy in small[1:]:
        copy.wait()
    loc = jnp.mod(columns_ref[...] - (b - 2) * ROWS, PANELS * ROWS)
    slot = g * SLOTS + lax.broadcasted_iota(jnp.int32, (SLOTS, ROWS), 0)
    live = slot < counts_ref[...].reshape(1, ROWS)
    shard, within = loc // SHARD, loc % SHARD
    row = shard * LEN + HEAD + within // 2 * BS
    entry = (shard * 128 + within) * 2 + within % 2
    code_ref[0:SLOTS, :] = jnp.where(live, row, HEAD)
    code_ref[SLOTS:, :] = jnp.where(live, entry, SPAN * GROUP * 256)
    load_a.wait()
    turn(a_ref, turned, blocks, 0)
    got(("F", "x"))
    to_y(F_PART, "F", 2, 1)
    keep.wait()
    to_z(F_PART, "F", 0, 1)
    got(("F", "y+", 2, 0), ("F", "y-", 2, 0))
    on_y(F_HALVES, "F", 2, 0)
    for dy in (-1, 1):
        to_z(F_PART, "F", dy, 0)
    got(("L", "x"))
    to_z(L_PART, "L", 0, 1)
    to_y(L_PART, "L", 2, 1)
    over((0, LEN), "A", 0, 1)
    got(("L", "y+", 2, 0), ("L", "y-", 2, 0))
    on_y(L_HALVES, "L", 2, 0)
    for dy in (-1, 1):
        over((0, LEN), "A", dy, 0)
    got(("L", "z+", 0, 0), ("L", "z-", 0, 0))
    for d in (0, 4):
        to_y(L_PART, "L", d, 0)
    over_far(L_PART, "L", 0, 0)
    turn(a_ref, turned, blocks, 128)
    got(("F", "y+", 2, 1), ("F", "y-", 2, 1))
    on_y(F_HALVES, "F", 2, 1)
    for dy in (-1, 1):
        to_z(F_PART, "F", dy, 1)
    got(("F", "f+", 2, 0), ("F", "f-", 2, 0))
    to_z(F_PART, "F", 2, 0)
    got(("L", "z+", 0, 1), ("L", "z-", 0, 1))
    for d in (0, 4):
        to_y(L_PART, "L", d, 1)
    over_far(L_PART, "L", 0, 1)
    got(("F", "f+", 2, 1), ("F", "f-", 2, 1))
    to_z(F_PART, "F", 2, 1)
    got(("L", "y+", 2, 1), ("L", "y-", 2, 1))
    on_y(L_HALVES, "L", 2, 1)
    for dy in (-1, 1):
        over((0, LEN), "A", dy, 1)
    turn(a_ref, turned, blocks, 256)
    got(("L", "f+", 2, 0), ("L", "f-", 2, 0))
    over((0, LEN), "A", 2, 0)
    got(("F", "z+", 0, 0), ("F", "z-", 0, 0))
    over_far(F_PART, "F", 0, 0)
    for d in (0, 4):
        got(("L", "y+", d, 0), ("L", "y-", d, 0))
        on_y(L_HALVES, "L", d, 0)
    for dy in (-1, 1):
        over_far(L_PART, "L", dy, 0)
    got(("L", "f+", 2, 1), ("L", "f-", 2, 1))
    over((0, LEN), "A", 2, 1)
    for shard in range(0, 2):
        left(win_ref, blocks, shard)
    got(("F", "z+", 0, 1), ("F", "z-", 0, 1))
    over_far(F_PART, "F", 0, 1)
    for dy in (-1, 1):
        got(("F", "z+", dy, 0), ("F", "z-", dy, 0))
        over_far(F_PART, "F", dy, 0)
        left(win_ref, blocks, 2 + (dy + 1) // 2)
    for d in (0, 4):
        got(("L", "y+", d, 1), ("L", "y-", d, 1))
        on_y(L_HALVES, "L", d, 1)
    for dy in (-1, 1):
        over_far(L_PART, "L", dy, 1)
    for n, (dy, dh) in enumerate(((-1, 1), (1, 1), (2, 0), (2, 1))):
        left(win_ref, blocks, 4 + n)
        settle()
        got(("F", "z+", dy, dh), ("F", "z-", dy, dh))
        over_far(F_PART, "F", dy, dh)
    for dh in (0, 1):
        for d in (0, 4):
            got(("L", "f+", d, dh), ("L", "f-", d, dh))
        over_far(L_PART, "L", 2, dh)
    for name in copies:
        if name[1] in ("s", "t"):
            got(name)
    for name in copies:
        if name not in settled:
            copies[name].wait_send()

    for n in range(SPAN * GROUP):
        near = win_ref[n // GROUP, n % GROUP, 0:HEAD, :].astype(F32)[0:1].astype(jnp.int32)
        table_ref[n : n + 1, :] = (near + n // GROUP * CB) * (2 * CB)
        if n // GROUP == 2:
            table_ref[n + 32 : n + 33, :] = near * 2
    table_ref[SPAN * GROUP : 48, :] = jnp.full((8, 128), TARGETS, jnp.int32)


COPIES = 86 - 8


def gathered(prolong, aggs, columns, counts, a):
    vmem, hbm = pl.BlockSpec(memory_space=pltpu.VMEM), pl.BlockSpec(memory_space=pltpu.HBM)
    return pl.pallas_call(
        gather_kernel,
        out_shape=(
            pltpu.VMEM((SPAN, GROUP, LEN, 2 * BS), BF16),
            pltpu.VMEM((ROWS, BS, 2 * BS), BF16),
            jax.ShapeDtypeStruct((2 * SLOTS, ROWS), jnp.int32),
            jax.ShapeDtypeStruct((56, 128), jnp.int32),
        ),
        in_specs=[hbm] * 5,
        out_specs=(vmem, vmem, vmem, vmem),
        scratch_shapes=[
            pltpu.VMEM((SHARD, BS, BS), BF16),
            pltpu.VMEM((LEN, 2 * BS), BF16),
            pltpu.VMEM((SLOTS, BS, BS, ROWS), BF16),
            pltpu.VMEM((BS * PITCH, 128), F32),
            pltpu.VMEM((SHARD,), jnp.int32),
            pltpu.VMEM((SLOTS, ROWS), jnp.int32),
            pltpu.VMEM((ROWS,), jnp.int32),
            pltpu.SemaphoreType.DMA((6,)),
            pltpu.SemaphoreType.DMA((COPIES,)),
            pltpu.SemaphoreType.DMA((COPIES,)),
        ],
        compiler_params=pltpu.CompilerParams(
            collective_id=0, has_side_effects=True, vmem_limit_bytes=20 * 2**20
        ),
        name="gather_window",
    )(*(pltpu.with_memory_space_constraint(x, pltpu.HBM) for x in (prolong, aggs, columns, counts, a)))


def compute_kernel(code_ref, table_ref, win_ref, blocks, part_ref, short_ref, acc):
    def clear(t, carry):
        acc[t] = jnp.zeros((BS, 2 * BS), F32)
        return carry

    lax.fori_loop(0, ACCS, clear, 0, unroll=8)

    for shard in range(GROUP):

        def right(j, carry, shard=shard):
            i = shard * SHARD + j
            none = jnp.zeros((BS, 2 * BS), BF16)
            column = table_ref[(48 + shard) * 128 + j]
            targets, picked = [], []
            for s in range(SLOTS):
                row = pl.multiple_of(code_ref[s, i], HEAD)
                entry = code_ref[SLOTS + s, i]
                picked.append(win_ref[pl.ds(row, BS), :])
                targets.append(table_ref[entry // 2] + column + entry % 2)
            stack = jnp.concatenate(
                [
                    jnp.concatenate([picked[0], none], axis=1),
                    jnp.concatenate([none, picked[1]], axis=1),
                ],
                axis=0,
            )
            r = jnp.dot(blocks[i], stack, preferred_element_type=F32)
            acc[targets[0]] += r[:, : 2 * BS]
            acc[targets[1]] += r[:, 2 * BS :]
            return carry

        lax.fori_loop(0, SHARD, right, 0, unroll=SHARD)

    low = lax.broadcasted_iota(jnp.int32, (BS, 2 * BS), 1) < BS

    def fold(t, carry):
        one, two = acc[4 * t], acc[4 * t + 1]
        three, four = acc[4 * t + 2], acc[4 * t + 3]
        first = one + pltpu.roll(two, BS, 1)
        second = pltpu.roll(three, BS, 1) + four
        place = t % GROUP * SPAN + t // GROUP
        block = jnp.where(low, first, second)
        part_ref[place] = block
        short_ref[place] = block.astype(BF16)
        return carry

    lax.fori_loop(0, BLOCKS, fold, 0, unroll=4)


def computed(codes, table, win, blocks):
    smem = pl.BlockSpec(memory_space=pltpu.SMEM)
    vmem = pl.BlockSpec(memory_space=pltpu.VMEM)
    return pl.pallas_call(
        compute_kernel,
        out_shape=(
            pltpu.VMEM((BLOCKS, BS, 2 * BS), F32),
            pltpu.VMEM((BLOCKS, BS, 2 * BS), BF16),
        ),
        in_specs=[smem, smem, vmem, vmem],
        out_specs=(vmem, vmem),
        scratch_shapes=[pltpu.VMEM((ACCS, BS, 2 * BS), F32)],
        compiler_params=pltpu.CompilerParams(vmem_limit_bytes=16 * 2**20),
        name="right_products",
    )(codes, table, win, blocks)


STEPS = ((2, 1, 1), (1, 1, 1), (3, 1, 1), (0, 1, 0), (2, 0, 1), (1, 0, 0), (3, 0, 0))


def reduce_kernel(
    part_ref, short_ref, out_ref, landed, landed_short, total, placed,
    send_sem, recv_sem, send2, recv2,
):
    b, g = lax.axis_index("blk"), lax.axis_index("grp")
    y, h = g // 2, g % 2
    others = [(y + dy) % CB * 2 + (h + dh) % 2 for dy, dh, _ in STEPS]
    barrier = pltpu.get_barrier_semaphore()
    for other in others:
        pl.semaphore_signal(barrier, inc=1, device_id=(b, other), device_id_type=MESH)
    pl.semaphore_wait(barrier, GROUP - 1)
    first, places = [], []
    for n, (other, (dy, dh, short)) in enumerate(zip(others, STEPS)):
        source, target = (short_ref, landed_short) if short else (part_ref, landed)
        place = target.at[sum(step[2] == short for step in STEPS[:n])]
        copy = pltpu.make_async_remote_copy(
            src_ref=source.at[pl.ds(other * SPAN, SPAN)],
            dst_ref=place,
            send_sem=send_sem.at[n],
            recv_sem=recv_sem.at[n],
            device_id=(b, other),
            device_id_type=MESH,
        )
        copy.start()
        first.append(copy)
        places.append(place)
    out_ref[...] = jnp.zeros(out_ref.shape, F32)
    total[...] = part_ref[pl.ds(g * SPAN, SPAN)]
    for copy, place in zip(first, places):
        copy.wait_recv()
        total[...] += place[...].astype(F32)

    def hop(d):
        panel = (b + PANELS - 2 + d) % PANELS
        owner, side = panel // 2, panel % 2
        copy = pltpu.make_async_remote_copy(
            src_ref=total.at[d],
            dst_ref=placed.at[side, g],
            send_sem=send2.at[d],
            recv_sem=recv2.at[side],
            device_id=(b, owner),
            device_id_type=MESH,
        )
        return owner, side, copy

    for d in range(SPAN):
        owner, side, copy = hop(d)

        @pl.when(owner != g)
        def _(copy=copy):
            copy.start()

        @pl.when(owner == g)
        def _(d=d, side=side):
            placed[side, g] = total[d]

    for side in range(2):
        d = (2 * g + side + PANELS + 2 - b) % PANELS

        @pl.when(d < SPAN)
        def _(side=side):
            rest = placed.at[side, pl.ds(0, GROUP - 1)]
            pltpu.make_async_remote_copy(
                src_ref=rest,
                dst_ref=rest,
                send_sem=send2.at[0],
                recv_sem=recv2.at[side],
                device_id=(b, others[0]),
                device_id_type=MESH,
            ).wait_recv()
            for n in range(GROUP):
                block = placed[side, n]
                row, column = side * CB + n // 2, n % 2 * 2
                out_ref[row, column] = block[:, :BS]
                out_ref[row, column + 1] = block[:, BS:]

    for d in range(SPAN):
        owner, side, copy = hop(d)

        @pl.when(owner != g)
        def _(copy=copy):
            copy.wait_send()

    for copy in first:
        copy.wait_send()


def reduced(part, short):
    vmem = pl.BlockSpec(memory_space=pltpu.VMEM)
    return pl.pallas_call(
        reduce_kernel,
        out_shape=jax.ShapeDtypeStruct((GROUP, CB, BS, BS), F32),
        in_specs=[vmem, vmem],
        out_specs=vmem,
        scratch_shapes=[
            pltpu.VMEM((GROUP // 2 - 1, SPAN, BS, 2 * BS), F32),
            pltpu.VMEM((GROUP // 2, SPAN, BS, 2 * BS), BF16),
            pltpu.VMEM((SPAN, BS, 2 * BS), F32),
            pltpu.VMEM((2, GROUP, BS, 2 * BS), F32),
            pltpu.SemaphoreType.DMA((GROUP - 1,)),
            pltpu.SemaphoreType.DMA((GROUP - 1,)),
            pltpu.SemaphoreType.DMA((SPAN,)),
            pltpu.SemaphoreType.DMA((2,)),
        ],
        compiler_params=pltpu.CompilerParams(
            collective_id=1, has_side_effects=True, vmem_limit_bytes=12 * 2**20
        ),
        name="reduce_blocks",
    )(part, short)


def local(block_values, block_columns, row_counts, prolong_blocks, aggregates):
    win, blocks, codes, table = gathered(
        prolong_blocks,
        aggregates,
        block_columns.T,
        row_counts,
        jnp.transpose(block_values, (1, 2, 3, 0)),
    )
    win = win.reshape(-1, 2 * BS)
    return reduced(*computed(codes, table.reshape(-1), win, blocks))


def solution(mesh):
    in_specs = (
        P("blk", "grp", None, None),
        P("blk", "grp"),
        P("blk"),
        P(("blk", "grp"), None, None),
        P(("blk", "grp")),
    )
    out_specs = P("grp", "blk", None, None)
    return jax.shard_map(local, mesh=mesh, in_specs=in_specs, out_specs=out_specs, check_vma=False)
```

```python
import functools

import jax
import jax.numpy as jnp
from jax import lax
from jax.experimental import pallas as pl
from jax.experimental.pallas import tpu as pltpu
from jax.sharding import PartitionSpec as P

MESH = pl.DeviceIdType.MESH
BF16, F32 = jnp.bfloat16, jnp.float32

BS = 64
CB = 4
ROWS = 384
SHARD = 48
PAIRS = SHARD // 2
PANELS = 16
GROUP = 8
SPAN = 5
HEAD = 16
LEN = HEAD + PAIRS * BS
CUT = HEAD + 13 * BS
F_PART, L_PART = (0, CUT), (CUT, LEN - CUT)
F_HALVES = ((0, 416), (416, CUT - 416))
L_HALVES = ((CUT, 352), (CUT + 352, 352))
SLOTS = 2
TARGETS = SPAN * CB * CB * 2
ACCS = TARGETS + 8
BLOCKS = TARGETS // 4
PITCH = 136


def turn(a_ref, turned, blocks, first):
    def over(r, carry):
        both = jnp.concatenate(
            [a_ref[s, r, :, first : first + 128] for s in range(SLOTS)], axis=0
        )
        start = pl.multiple_of(r * PITCH, 8)
        turned[pl.ds(start, 128), :] = both.T.astype(F32)
        return carry

    lax.fori_loop(0, BS, over, 0, unroll=16)

    def collect(i, carry):
        blocks[first + i] = turned[pl.ds(i, BS, stride=PITCH), :].astype(BF16)
        return carry

    lax.fori_loop(0, 128, collect, 0, unroll=16)


def left(win_ref, blocks, shard):
    def pair(j, carry):
        start = pl.multiple_of(HEAD + j * BS, HEAD)
        both = win_ref[2, shard, pl.ds(start, BS), :].T
        for half in range(2):
            i = shard * SHARD + 2 * j + half
            t = jnp.dot(
                both[half * BS : (half + 1) * BS, :], blocks[i], preferred_element_type=F32
            )
            blocks[i] = t.astype(BF16)
        return carry

    lax.fori_loop(0, PAIRS, pair, 0, unroll=12)


def gather_kernel(
    p_ref, agg_hbm, columns_hbm, counts_hbm, a_hbm,
    win_ref, blocks, code_ref, target_ref,
    raw, own, a_ref, turned, agg_ref, columns_ref, counts_ref, shards, withins,
    local_sem, send_sem, recv_sem,
):
    b, g = lax.axis_index("blk"), lax.axis_index("grp")
    core = b % 2
    y, h = g // 2, g % 2
    other = g + 1 - 2 * h
    z = (b // 2) % 4
    up_end = jnp.where(z == 3, 1, 0)
    down_end = jnp.where(z == 0, 1, 0)

    def on_k(step, end, dh):
        return (b + step + PANELS) % PANELS, g + dh * end * (1 - 2 * h)

    up_y, down_y = (b, (g + 2) % GROUP), (b, (g + GROUP - 2) % GROUP)
    across, sibling = (b, other), (b + 1 - 2 * core, g)

    load = pltpu.make_async_copy(p_ref, raw, local_sem.at[0])
    load.start()
    small = [
        pltpu.make_async_copy(source, target, local_sem.at[3 + n])
        for n, (source, target) in enumerate(
            ((agg_hbm, agg_ref), (columns_hbm, columns_ref), (counts_hbm, counts_ref))
        )
    ]
    for copy in small:
        copy.start()
    barrier = pltpu.get_barrier_semaphore()
    greeted = [up_y, down_y, across, sibling]
    for step in (2, PANELS - 2):
        greeted += [((b + step) % PANELS, column) for column in (g, other)]
    for device in greeted:
        pl.semaphore_signal(barrier, inc=1, device_id=device, device_id_type=MESH)
    small[0].wait()
    own[0:HEAD, :] = jnp.zeros((HEAD, 2 * BS), BF16)
    own[0:HEAD, 0:SHARD] = jnp.broadcast_to(
        (agg_ref[...] % CB).astype(F32).reshape(1, SHARD), (HEAD, SHARD)
    ).astype(BF16)
    load.wait()
    load_a = pltpu.make_async_copy(a_hbm, a_ref, local_sem.at[2])
    load_a.start()

    def pack(j, carry):
        row = pl.multiple_of(HEAD + j * BS, HEAD)
        own[pl.ds(row, BS), :] = jnp.concatenate([raw[2 * j], raw[2 * j + 1]], axis=-1)
        return carry

    lax.fori_loop(0, PAIRS, pack, 0, unroll=8)
    keep = pltpu.make_async_copy(own, win_ref.at[2, g], local_sem.at[1])
    keep.start()
    pl.semaphore_wait(barrier, len(greeted))

    copies, arrived, settled = {}, [], set()

    def at(d, dy, dh):
        return win_ref.at[d, ((y + dy) % 4) * 2 + (h + dh) % 2]

    def send(name, part, d, dy, dh, to_d, device, src=None):
        start, size = part
        piece = pl.ds(start, size)
        n = len(copies)
        source = own if src is not None else at(d, dy, dh)
        copies[name] = pltpu.make_async_remote_copy(
            src_ref=source.at[piece, :],
            dst_ref=at(to_d, dy, dh).at[piece, :],
            send_sem=send_sem.at[n],
            recv_sem=recv_sem.at[n],
            device_id=device,
            device_id_type=MESH,
        )
        copies[name].start()

    def got(*names):
        for name in names:
            copies[name].wait_recv()
            arrived.append(name)

    def settle():
        for name in arrived:
            if name not in settled:
                settled.add(name)
                copies[name].wait_send()

    def to_y(part, tag, d, dh, src=None):
        send((tag, "y+", d, dh), part, d, 0, dh, d, up_y, src)
        send((tag, "y-", d, dh), part, d, 0, dh, d, down_y, src)

    def on_y(halves, tag, d, dh):
        send((tag, "f+", d, dh), halves[0], d, -1, dh, d, up_y)
        send((tag, "f-", d, dh), halves[1], d, 1, dh, d, down_y)

    def to_z(part, tag, dy, dh, src=None):
        for sign, step, end, to_d in (("z+", 2, up_end, 0), ("z-", -2, down_end, 4)):
            column = dh * (1 - end)
            send((tag, sign, dy, dh), part, 2, dy, column, to_d, on_k(step, end, dh), src)

    def over(part, tag, dy, dh, src=None):
        send((tag, "s", dy, dh), part, 2, dy, dh, 1 + 2 * core, sibling, src)

    def over_far(part, tag, dy, dh):
        send((tag, "t", dy, dh), part, 4 - 4 * core, dy, dh, 3 - 2 * core, sibling)

    send(("F", "x"), F_PART, 2, 0, 0, 2, across, own)
    to_y(F_PART, "F", 2, 0, own)
    to_z(F_PART, "F", 0, 0, own)
    send(("L", "x"), L_PART, 2, 0, 0, 2, across, own)
    to_z(L_PART, "L", 0, 0, own)
    to_y(L_PART, "L", 2, 0, own)
    over((0, LEN), "A", 0, 0, own)

    for copy in small[1:]:
        copy.wait()
    loc = jnp.mod(columns_ref[...] - (b - 2) * ROWS, PANELS * ROWS)
    slot = g * SLOTS + lax.broadcasted_iota(jnp.int32, (SLOTS, ROWS), 0)
    live = slot < counts_ref[...].reshape(1, ROWS)
    shard, within = loc // SHARD, loc % SHARD
    row = jnp.where(live, shard * LEN + HEAD + within // 2 * BS, HEAD)
    shard = jnp.where(live, shard, SPAN * GROUP)
    for value, target in ((row, code_ref), (shard, shards), (within, withins)):
        target[...] = jnp.zeros((8, 128), jnp.int32)
        for c in range(ROWS // 128):
            target[2 * c : 2 * c + 2, :] = value[:, c * 128 : (c + 1) * 128]
    load_a.wait()
    turn(a_ref, turned, blocks, 0)
    got(("F", "x"))
    to_y(F_PART, "F", 2, 1)
    keep.wait()
    to_z(F_PART, "F", 0, 1)
    got(("F", "y+", 2, 0), ("F", "y-", 2, 0))
    on_y(F_HALVES, "F", 2, 0)
    for dy in (-1, 1):
        to_z(F_PART, "F", dy, 0)
    got(("L", "x"))
    to_z(L_PART, "L", 0, 1)
    to_y(L_PART, "L", 2, 1)
    over((0, LEN), "A", 0, 1)
    got(("L", "y+", 2, 0), ("L", "y-", 2, 0))
    on_y(L_HALVES, "L", 2, 0)
    for dy in (-1, 1):
        over((0, LEN), "A", dy, 0)
    got(("L", "z+", 0, 0), ("L", "z-", 0, 0))
    for d in (0, 4):
        to_y(L_PART, "L", d, 0)
    over_far(L_PART, "L", 0, 0)
    turn(a_ref, turned, blocks, 128)
    got(("F", "y+", 2, 1), ("F", "y-", 2, 1))
    on_y(F_HALVES, "F", 2, 1)
    for dy in (-1, 1):
        to_z(F_PART, "F", dy, 1)
    got(("F", "f+", 2, 0), ("F", "f-", 2, 0))
    to_z(F_PART, "F", 2, 0)
    got(("L", "z+", 0, 1), ("L", "z-", 0, 1))
    for d in (0, 4):
        to_y(L_PART, "L", d, 1)
    over_far(L_PART, "L", 0, 1)
    got(("F", "f+", 2, 1), ("F", "f-", 2, 1))
    to_z(F_PART, "F", 2, 1)
    got(("L", "y+", 2, 1), ("L", "y-", 2, 1))
    on_y(L_HALVES, "L", 2, 1)
    for dy in (-1, 1):
        over((0, LEN), "A", dy, 1)
    turn(a_ref, turned, blocks, 256)
    got(("L", "f+", 2, 0), ("L", "f-", 2, 0))
    over((0, LEN), "A", 2, 0)
    got(("F", "z+", 0, 0), ("F", "z-", 0, 0))
    over_far(F_PART, "F", 0, 0)
    for d in (0, 4):
        got(("L", "y+", d, 0), ("L", "y-", d, 0))
        on_y(L_HALVES, "L", d, 0)
    for dy in (-1, 1):
        over_far(L_PART, "L", dy, 0)
    got(("L", "f+", 2, 1), ("L", "f-", 2, 1))
    over((0, LEN), "A", 2, 1)
    for shard in range(0, 2):
        left(win_ref, blocks, shard)
    got(("F", "z+", 0, 1), ("F", "z-", 0, 1))
    over_far(F_PART, "F", 0, 1)
    for dy in (-1, 1):
        got(("F", "z+", dy, 0), ("F", "z-", dy, 0))
        over_far(F_PART, "F", dy, 0)
        left(win_ref, blocks, 2 + (dy + 1) // 2)
    for d in (0, 4):
        got(("L", "y+", d, 1), ("L", "y-", d, 1))
        on_y(L_HALVES, "L", d, 1)
    for dy in (-1, 1):
        over_far(L_PART, "L", dy, 1)
    for n, (dy, dh) in enumerate(((-1, 1), (1, 1), (2, 0), (2, 1))):
        left(win_ref, blocks, 4 + n)
        settle()
        got(("F", "z+", dy, dh), ("F", "z-", dy, dh))
        over_far(F_PART, "F", dy, dh)
    for dh in (0, 1):
        for d in (0, 4):
            got(("L", "f+", d, dh), ("L", "f-", d, dh))
        over_far(L_PART, "L", 2, dh)
    for name in copies:
        if name[1] in ("s", "t"):
            got(name)
    for name in copies:
        if name not in settled:
            copies[name].wait_send()

    place = lax.broadcasted_iota(jnp.int32, (8, 128), 0) // 2 * 128
    place += lax.broadcasted_iota(jnp.int32, (8, 128), 1)
    shard, within = shards[...], withins[...]
    target = jnp.full((8, 128), TARGETS, jnp.int32)
    column = jnp.zeros((8, 128), jnp.int32)

    def look(value, index):
        table = jnp.broadcast_to(value, (8, 128))
        return jnp.take_along_axis(table, index, axis=1, mode="promise_in_bounds")

    for n in range(SPAN * GROUP):
        d = n // GROUP
        near = win_ref[d, n % GROUP, 0:HEAD, :].astype(F32)[0:1].astype(jnp.int32)
        found = look((near + d * CB) * (2 * CB), within)
        target = jnp.where(shard == n, found, target)
        if d == 2:
            found = look(near * 2, place % SHARD)
            column = jnp.where(place // SHARD == n % GROUP, found, column)
    target_ref[...] = target + column + within % 2


COPIES = 86 - 8


def gathered(prolong, aggs, columns, counts, a):
    vmem, hbm = pl.BlockSpec(memory_space=pltpu.VMEM), pl.BlockSpec(memory_space=pltpu.HBM)
    return pl.pallas_call(
        gather_kernel,
        out_shape=(
            pltpu.VMEM((SPAN, GROUP, LEN, 2 * BS), BF16),
            pltpu.VMEM((ROWS, BS, 2 * BS), BF16),
            jax.ShapeDtypeStruct((8, 128), jnp.int32),
            jax.ShapeDtypeStruct((8, 128), jnp.int32),
        ),
        in_specs=[hbm] * 5,
        out_specs=(vmem, vmem, vmem, vmem),
        scratch_shapes=[
            pltpu.VMEM((SHARD, BS, BS), BF16),
            pltpu.VMEM((LEN, 2 * BS), BF16),
            pltpu.VMEM((SLOTS, BS, BS, ROWS), BF16),
            pltpu.VMEM((BS * PITCH, 128), F32),
            pltpu.VMEM((SHARD,), jnp.int32),
            pltpu.VMEM((SLOTS, ROWS), jnp.int32),
            pltpu.VMEM((ROWS,), jnp.int32),
            pltpu.VMEM((8, 128), jnp.int32),
            pltpu.VMEM((8, 128), jnp.int32),
            pltpu.SemaphoreType.DMA((6,)),
            pltpu.SemaphoreType.DMA((COPIES,)),
            pltpu.SemaphoreType.DMA((COPIES,)),
        ],
        compiler_params=pltpu.CompilerParams(
            collective_id=0, has_side_effects=True, vmem_limit_bytes=20 * 2**20
        ),
        name="gather_window",
    )(*(pltpu.with_memory_space_constraint(x, pltpu.HBM) for x in (prolong, aggs, columns, counts, a)))


def right_kernel(code_ref, target_ref, win_ref, blocks, acc):
    def clear(t, carry):
        acc[t] = jnp.zeros((BS, 2 * BS), F32)
        return carry

    lax.fori_loop(0, ACCS, clear, 0, unroll=8)

    for shard in range(GROUP):

        def right(j, carry, shard=shard):
            i = shard * SHARD + j
            none = jnp.zeros((BS, 2 * BS), BF16)
            targets, picked = [], []
            for s in range(SLOTS):
                entry = i // 128 * 2 + s, i % 128
                row = pl.multiple_of(code_ref[entry], HEAD)
                picked.append(win_ref[pl.ds(row, BS), :])
                targets.append(target_ref[entry])
            stack = jnp.concatenate(
                [
                    jnp.concatenate([picked[0], none], axis=1),
                    jnp.concatenate([none, picked[1]], axis=1),
                ],
                axis=0,
            )
            r = jnp.dot(blocks[i], stack, preferred_element_type=F32)
            acc[targets[0]] += r[:, : 2 * BS]
            acc[targets[1]] += r[:, 2 * BS :]
            return carry

        lax.fori_loop(0, SHARD, right, 0, unroll=SHARD)


def multiplied(codes, targets, win, blocks):
    smem = pl.BlockSpec(memory_space=pltpu.SMEM)
    vmem = pl.BlockSpec(memory_space=pltpu.VMEM)
    return pl.pallas_call(
        right_kernel,
        out_shape=pltpu.VMEM((ACCS, BS, 2 * BS), F32),
        in_specs=[smem, smem, vmem, vmem],
        out_specs=vmem,
        compiler_params=pltpu.CompilerParams(vmem_limit_bytes=8 * 2**20),
        name="right_products",
    )(codes, targets, win, blocks)


STEPS = ((2, 1, 1), (1, 1, 1), (3, 1, 1), (0, 1, 0), (2, 0, 1), (1, 0, 0), (3, 0, 0))


def reduce_kernel(
    acc, out_ref, part_ref, short_ref, landed, landed_short, total, placed,
    send_sem, recv_sem, send2, recv2,
):
    b, g = lax.axis_index("blk"), lax.axis_index("grp")
    y, h = g // 2, g % 2
    others = [(y + dy) % CB * 2 + (h + dh) % 2 for dy, dh, _ in STEPS]
    barrier = pltpu.get_barrier_semaphore()
    for other in others:
        pl.semaphore_signal(barrier, inc=1, device_id=(b, other), device_id_type=MESH)

    low = lax.broadcasted_iota(jnp.int32, (BS, 2 * BS), 1) < BS

    def fold(t, carry):
        one, two = acc[4 * t], acc[4 * t + 1]
        three, four = acc[4 * t + 2], acc[4 * t + 3]
        first = one + pltpu.roll(two, BS, 1)
        second = pltpu.roll(three, BS, 1) + four
        place = t % GROUP * SPAN + t // GROUP
        block = jnp.where(low, first, second)
        part_ref[place] = block
        short_ref[place] = block.astype(BF16)
        return carry

    lax.fori_loop(0, BLOCKS, fold, 0, unroll=8)
    pl.semaphore_wait(barrier, GROUP - 1)
    first, places = [], []
    for n, (other, (dy, dh, short)) in enumerate(zip(others, STEPS)):
        source, target = (short_ref, landed_short) if short else (part_ref, landed)
        place = target.at[sum(step[2] == short for step in STEPS[:n])]
        copy = pltpu.make_async_remote_copy(
            src_ref=source.at[pl.ds(other * SPAN, SPAN)],
            dst_ref=place,
            send_sem=send_sem.at[n],
            recv_sem=recv_sem.at[n],
            device_id=(b, other),
            device_id_type=MESH,
        )
        copy.start()
        first.append(copy)
        places.append(place)
    out_ref[...] = jnp.zeros(out_ref.shape, F32)
    total[...] = part_ref[pl.ds(g * SPAN, SPAN)]
    for copy, place in zip(first, places):
        copy.wait_recv()
        total[...] += place[...].astype(F32)

    def hop(d):
        panel = (b + PANELS - 2 + d) % PANELS
        owner, side = panel // 2, panel % 2
        copy = pltpu.make_async_remote_copy(
            src_ref=total.at[d],
            dst_ref=placed.at[side, g],
            send_sem=send2.at[d],
            recv_sem=recv2.at[side],
            device_id=(b, owner),
            device_id_type=MESH,
        )
        return owner, side, copy

    for d in range(SPAN):
        owner, side, copy = hop(d)

        @pl.when(owner != g)
        def _(copy=copy):
            copy.start()

        @pl.when(owner == g)
        def _(d=d, side=side):
            placed[side, g] = total[d]

    for side in range(2):
        d = (2 * g + side + PANELS + 2 - b) % PANELS

        @pl.when(d < SPAN)
        def _(side=side):
            rest = placed.at[side, pl.ds(0, GROUP - 1)]
            pltpu.make_async_remote_copy(
                src_ref=rest,
                dst_ref=rest,
                send_sem=send2.at[0],
                recv_sem=recv2.at[side],
                device_id=(b, others[0]),
                device_id_type=MESH,
            ).wait_recv()
            for n in range(GROUP):
                block = placed[side, n]
                row, column = side * CB + n // 2, n % 2 * 2
                out_ref[row, column] = block[:, :BS]
                out_ref[row, column + 1] = block[:, BS:]

    for d in range(SPAN):
        owner, side, copy = hop(d)

        @pl.when(owner != g)
        def _(copy=copy):
            copy.wait_send()

    for copy in first:
        copy.wait_send()


def reduced(acc):
    vmem = pl.BlockSpec(memory_space=pltpu.VMEM)
    return pl.pallas_call(
        reduce_kernel,
        out_shape=jax.ShapeDtypeStruct((GROUP, CB, BS, BS), F32),
        in_specs=[vmem],
        out_specs=vmem,
        scratch_shapes=[
            pltpu.VMEM((BLOCKS, BS, 2 * BS), F32),
            pltpu.VMEM((BLOCKS, BS, 2 * BS), BF16),
            pltpu.VMEM((GROUP // 2 - 1, SPAN, BS, 2 * BS), F32),
            pltpu.VMEM((GROUP // 2, SPAN, BS, 2 * BS), BF16),
            pltpu.VMEM((SPAN, BS, 2 * BS), F32),
            pltpu.VMEM((2, GROUP, BS, 2 * BS), F32),
            pltpu.SemaphoreType.DMA((GROUP - 1,)),
            pltpu.SemaphoreType.DMA((GROUP - 1,)),
            pltpu.SemaphoreType.DMA((SPAN,)),
            pltpu.SemaphoreType.DMA((2,)),
        ],
        compiler_params=pltpu.CompilerParams(
            collective_id=1, has_side_effects=True, vmem_limit_bytes=12 * 2**20
        ),
        name="reduce_blocks",
    )(acc)


def local(block_values, block_columns, row_counts, prolong_blocks, aggregates):
    win, blocks, codes, targets = gathered(
        prolong_blocks,
        aggregates,
        block_columns.T,
        row_counts,
        jnp.transpose(block_values, (1, 2, 3, 0)),
    )
    win = win.reshape(-1, 2 * BS)
    return reduced(multiplied(codes, targets, win, blocks))


def solution(mesh):
    in_specs = (
        P("blk", "grp", None, None),
        P("blk", "grp"),
        P("blk"),
        P(("blk", "grp"), None, None),
        P(("blk", "grp")),
    )
    out_specs = P("grp", "blk", None, None)
    return jax.shard_map(local, mesh=mesh, in_specs=in_specs, out_specs=out_specs, check_vma=False)
```

```python
import functools

import jax
import jax.numpy as jnp
from jax import lax
from jax.experimental import pallas as pl
from jax.experimental.pallas import tpu as pltpu
from jax.sharding import PartitionSpec as P

MESH = pl.DeviceIdType.MESH
BF16, F32 = jnp.bfloat16, jnp.float32

BS = 64
CB = 4
ROWS = 384
SHARD = 48
PAIRS = SHARD // 2
PANELS = 16
GROUP = 8
SPAN = 5
HEAD = 16
LEN = HEAD + PAIRS * BS
CUT = HEAD + 13 * BS
F_PART, L_PART = (0, CUT), (CUT, LEN - CUT)
F_HALVES = ((0, 416), (416, CUT - 416))
L_HALVES = ((CUT, 352), (CUT + 352, 352))
SLOTS = 2
TARGETS = SPAN * CB * CB * 2
ACCS = TARGETS + 8
BLOCKS = TARGETS // 4
PITCH = 136


def turn(a_ref, turned, blocks, first):
    def over(r, carry):
        both = jnp.concatenate(
            [a_ref[s, r, :, first : first + 128] for s in range(SLOTS)], axis=0
        )
        start = pl.multiple_of(r * PITCH, 8)
        turned[pl.ds(start, 128), :] = both.T.astype(F32)
        return carry

    lax.fori_loop(0, BS, over, 0, unroll=16)

    def collect(i, carry):
        blocks[first + i] = turned[pl.ds(i, BS, stride=PITCH), :].astype(BF16)
        return carry

    lax.fori_loop(0, 128, collect, 0, unroll=16)


def left(win_ref, blocks, lows, shard):
    def pair(j, carry):
        start = pl.multiple_of(HEAD + j * BS, HEAD)
        both = win_ref[2, shard, pl.ds(start, BS), :].T
        for half in range(2):
            i = shard * SHARD + 2 * j + half
            t = jnp.dot(
                both[half * BS : (half + 1) * BS, :], blocks[i], preferred_element_type=F32
            )
            high = t.astype(BF16)
            blocks[i] = high
            lows[i] = (t - high.astype(F32)).astype(BF16)
        return carry

    lax.fori_loop(0, PAIRS, pair, 0, unroll=12)


def gather_kernel(
    p_ref, agg_hbm, columns_hbm, counts_hbm, a_hbm,
    win_ref, blocks, lows, code_ref, target_ref,
    raw, own, a_ref, turned, agg_ref, columns_ref, counts_ref, shards, withins,
    local_sem, send_sem, recv_sem,
):
    b, g = lax.axis_index("blk"), lax.axis_index("grp")
    core = b % 2
    y, h = g // 2, g % 2
    other = g + 1 - 2 * h
    z = (b // 2) % 4
    up_end = jnp.where(z == 3, 1, 0)
    down_end = jnp.where(z == 0, 1, 0)

    def on_k(step, end, dh):
        return (b + step + PANELS) % PANELS, g + dh * end * (1 - 2 * h)

    up_y, down_y = (b, (g + 2) % GROUP), (b, (g + GROUP - 2) % GROUP)
    across, sibling = (b, other), (b + 1 - 2 * core, g)

    load = pltpu.make_async_copy(p_ref, raw, local_sem.at[0])
    load.start()
    small = [
        pltpu.make_async_copy(source, target, local_sem.at[3 + n])
        for n, (source, target) in enumerate(
            ((agg_hbm, agg_ref), (columns_hbm, columns_ref), (counts_hbm, counts_ref))
        )
    ]
    for copy in small:
        copy.start()
    barrier = pltpu.get_barrier_semaphore()
    greeted = [up_y, down_y, across, sibling]
    for step in (2, PANELS - 2):
        greeted += [((b + step) % PANELS, column) for column in (g, other)]
    for device in greeted:
        pl.semaphore_signal(barrier, inc=1, device_id=device, device_id_type=MESH)
    small[0].wait()
    own[0:HEAD, :] = jnp.zeros((HEAD, 2 * BS), BF16)
    own[0:HEAD, 0:SHARD] = jnp.broadcast_to(
        (agg_ref[...] % CB).astype(F32).reshape(1, SHARD), (HEAD, SHARD)
    ).astype(BF16)
    load.wait()
    load_a = pltpu.make_async_copy(a_hbm, a_ref, local_sem.at[2])
    load_a.start()

    def pack(j, carry):
        row = pl.multiple_of(HEAD + j * BS, HEAD)
        own[pl.ds(row, BS), :] = jnp.concatenate([raw[2 * j], raw[2 * j + 1]], axis=-1)
        return carry

    lax.fori_loop(0, PAIRS, pack, 0, unroll=8)
    keep = pltpu.make_async_copy(own, win_ref.at[2, g], local_sem.at[1])
    keep.start()
    pl.semaphore_wait(barrier, len(greeted))

    copies, arrived, settled = {}, [], set()

    def at(d, dy, dh):
        return win_ref.at[d, ((y + dy) % 4) * 2 + (h + dh) % 2]

    def send(name, part, d, dy, dh, to_d, device, src=None):
        start, size = part
        piece = pl.ds(start, size)
        n = len(copies)
        source = own if src is not None else at(d, dy, dh)
        copies[name] = pltpu.make_async_remote_copy(
            src_ref=source.at[piece, :],
            dst_ref=at(to_d, dy, dh).at[piece, :],
            send_sem=send_sem.at[n],
            recv_sem=recv_sem.at[n],
            device_id=device,
            device_id_type=MESH,
        )
        copies[name].start()

    def got(*names):
        for name in names:
            copies[name].wait_recv()
            arrived.append(name)

    def settle():
        for name in arrived:
            if name not in settled:
                settled.add(name)
                copies[name].wait_send()

    def to_y(part, tag, d, dh, src=None):
        send((tag, "y+", d, dh), part, d, 0, dh, d, up_y, src)
        send((tag, "y-", d, dh), part, d, 0, dh, d, down_y, src)

    def on_y(halves, tag, d, dh):
        send((tag, "f+", d, dh), halves[0], d, -1, dh, d, up_y)
        send((tag, "f-", d, dh), halves[1], d, 1, dh, d, down_y)

    def to_z(part, tag, dy, dh, src=None):
        for sign, step, end, to_d in (("z+", 2, up_end, 0), ("z-", -2, down_end, 4)):
            column = dh * (1 - end)
            send((tag, sign, dy, dh), part, 2, dy, column, to_d, on_k(step, end, dh), src)

    def over(part, tag, dy, dh, src=None):
        send((tag, "s", dy, dh), part, 2, dy, dh, 1 + 2 * core, sibling, src)

    def over_far(part, tag, dy, dh):
        send((tag, "t", dy, dh), part, 4 - 4 * core, dy, dh, 3 - 2 * core, sibling)

    send(("F", "x"), F_PART, 2, 0, 0, 2, across, own)
    to_y(F_PART, "F", 2, 0, own)
    to_z(F_PART, "F", 0, 0, own)
    send(("L", "x"), L_PART, 2, 0, 0, 2, across, own)
    to_z(L_PART, "L", 0, 0, own)
    to_y(L_PART, "L", 2, 0, own)
    over((0, LEN), "A", 0, 0, own)

    for copy in small[1:]:
        copy.wait()
    loc = jnp.mod(columns_ref[...] - (b - 2) * ROWS, PANELS * ROWS)
    slot = g * SLOTS + lax.broadcasted_iota(jnp.int32, (SLOTS, ROWS), 0)
    live = slot < counts_ref[...].reshape(1, ROWS)
    shard, within = loc // SHARD, loc % SHARD
    row = jnp.where(live, shard * LEN + HEAD + within // 2 * BS, HEAD)
    shard = jnp.where(live, shard, SPAN * GROUP)
    for value, target in ((row, code_ref), (shard, shards), (within, withins)):
        target[...] = jnp.zeros((8, 128), jnp.int32)
        for c in range(ROWS // 128):
            target[2 * c : 2 * c + 2, :] = value[:, c * 128 : (c + 1) * 128]
    load_a.wait()
    turn(a_ref, turned, blocks, 0)
    got(("F", "x"))
    to_y(F_PART, "F", 2, 1)
    keep.wait()
    to_z(F_PART, "F", 0, 1)
    got(("F", "y+", 2, 0), ("F", "y-", 2, 0))
    on_y(F_HALVES, "F", 2, 0)
    for dy in (-1, 1):
        to_z(F_PART, "F", dy, 0)
    got(("L", "x"))
    to_z(L_PART, "L", 0, 1)
    to_y(L_PART, "L", 2, 1)
    over((0, LEN), "A", 0, 1)
    got(("L", "y+", 2, 0), ("L", "y-", 2, 0))
    on_y(L_HALVES, "L", 2, 0)
    for dy in (-1, 1):
        over((0, LEN), "A", dy, 0)
    got(("L", "z+", 0, 0), ("L", "z-", 0, 0))
    for d in (0, 4):
        to_y(L_PART, "L", d, 0)
    over_far(L_PART, "L", 0, 0)
    turn(a_ref, turned, blocks, 128)
    got(("F", "y+", 2, 1), ("F", "y-", 2, 1))
    on_y(F_HALVES, "F", 2, 1)
    for dy in (-1, 1):
        to_z(F_PART, "F", dy, 1)
    got(("F", "f+", 2, 0), ("F", "f-", 2, 0))
    to_z(F_PART, "F", 2, 0)
    got(("L", "z+", 0, 1), ("L", "z-", 0, 1))
    for d in (0, 4):
        to_y(L_PART, "L", d, 1)
    over_far(L_PART, "L", 0, 1)
    got(("F", "f+", 2, 1), ("F", "f-", 2, 1))
    to_z(F_PART, "F", 2, 1)
    got(("L", "y+", 2, 1), ("L", "y-", 2, 1))
    on_y(L_HALVES, "L", 2, 1)
    for dy in (-1, 1):
        over((0, LEN), "A", dy, 1)
    turn(a_ref, turned, blocks, 256)
    got(("L", "f+", 2, 0), ("L", "f-", 2, 0))
    over((0, LEN), "A", 2, 0)
    got(("F", "z+", 0, 0), ("F", "z-", 0, 0))
    over_far(F_PART, "F", 0, 0)
    for d in (0, 4):
        got(("L", "y+", d, 0), ("L", "y-", d, 0))
        on_y(L_HALVES, "L", d, 0)
    for dy in (-1, 1):
        over_far(L_PART, "L", dy, 0)
    got(("L", "f+", 2, 1), ("L", "f-", 2, 1))
    over((0, LEN), "A", 2, 1)
    for shard in range(0, 2):
        left(win_ref, blocks, lows, shard)
    got(("F", "z+", 0, 1), ("F", "z-", 0, 1))
    over_far(F_PART, "F", 0, 1)
    for dy in (-1, 1):
        got(("F", "z+", dy, 0), ("F", "z-", dy, 0))
        over_far(F_PART, "F", dy, 0)
        left(win_ref, blocks, lows, 2 + (dy + 1) // 2)
    for d in (0, 4):
        got(("L", "y+", d, 1), ("L", "y-", d, 1))
        on_y(L_HALVES, "L", d, 1)
    for dy in (-1, 1):
        over_far(L_PART, "L", dy, 1)
    for n, (dy, dh) in enumerate(((-1, 1), (1, 1), (2, 0), (2, 1))):
        left(win_ref, blocks, lows, 4 + n)
        settle()
        got(("F", "z+", dy, dh), ("F", "z-", dy, dh))
        over_far(F_PART, "F", dy, dh)
    for dh in (0, 1):
        for d in (0, 4):
            got(("L", "f+", d, dh), ("L", "f-", d, dh))
        over_far(L_PART, "L", 2, dh)
    for name in copies:
        if name[1] in ("s", "t"):
            got(name)
    for name in copies:
        if name not in settled:
            copies[name].wait_send()

    place = lax.broadcasted_iota(jnp.int32, (8, 128), 0) // 2 * 128
    place += lax.broadcasted_iota(jnp.int32, (8, 128), 1)
    shard, within = shards[...], withins[...]
    target = jnp.full((8, 128), TARGETS, jnp.int32)
    column = jnp.zeros((8, 128), jnp.int32)

    def look(value, index):
        table = jnp.broadcast_to(value, (8, 128))
        return jnp.take_along_axis(table, index, axis=1, mode="promise_in_bounds")

    for n in range(SPAN * GROUP):
        d = n // GROUP
        near = win_ref[d, n % GROUP, 0:HEAD, :].astype(F32)[0:1].astype(jnp.int32)
        found = look((near + d * CB) * (2 * CB), within)
        target = jnp.where(shard == n, found, target)
        if d == 2:
            found = look(near * 2, place % SHARD)
            column = jnp.where(place // SHARD == n % GROUP, found, column)
    target_ref[...] = target + column + within % 2


COPIES = 86 - 8


def gathered(prolong, aggs, columns, counts, a):
    vmem, hbm = pl.BlockSpec(memory_space=pltpu.VMEM), pl.BlockSpec(memory_space=pltpu.HBM)
    return pl.pallas_call(
        gather_kernel,
        out_shape=(
            pltpu.VMEM((SPAN, GROUP, LEN, 2 * BS), BF16),
            pltpu.VMEM((ROWS, BS, 2 * BS), BF16),
            pltpu.VMEM((ROWS, BS, 2 * BS), BF16),
            jax.ShapeDtypeStruct((8, 128), jnp.int32),
            jax.ShapeDtypeStruct((8, 128), jnp.int32),
        ),
        in_specs=[hbm] * 5,
        out_specs=(vmem,) * 5,
        scratch_shapes=[
            pltpu.VMEM((SHARD, BS, BS), BF16),
            pltpu.VMEM((LEN, 2 * BS), BF16),
            pltpu.VMEM((SLOTS, BS, BS, ROWS), BF16),
            pltpu.VMEM((BS * PITCH, 128), F32),
            pltpu.VMEM((SHARD,), jnp.int32),
            pltpu.VMEM((SLOTS, ROWS), jnp.int32),
            pltpu.VMEM((ROWS,), jnp.int32),
            pltpu.VMEM((8, 128), jnp.int32),
            pltpu.VMEM((8, 128), jnp.int32),
            pltpu.SemaphoreType.DMA((6,)),
            pltpu.SemaphoreType.DMA((COPIES,)),
            pltpu.SemaphoreType.DMA((COPIES,)),
        ],
        compiler_params=pltpu.CompilerParams(
            collective_id=0, has_side_effects=True, vmem_limit_bytes=20 * 2**20
        ),
        name="gather_window",
    )(*(pltpu.with_memory_space_constraint(x, pltpu.HBM) for x in (prolong, aggs, columns, counts, a)))


def right_kernel(code_ref, target_ref, win_ref, blocks, lows, acc_one, acc_two):
    def clear(t, carry):
        acc_one[t] = jnp.zeros((BS, 2 * BS), F32)
        acc_two[t] = jnp.zeros((BS, 2 * BS), F32)
        return carry

    lax.fori_loop(0, ACCS, clear, 0, unroll=8)

    for shard in range(GROUP):

        def right(j, carry, shard=shard):
            i = shard * SHARD + j
            none = jnp.zeros((BS, 2 * BS), BF16)
            targets, picked = [], []
            for s in range(SLOTS):
                entry = i // 128 * 2 + s, i % 128
                row = pl.multiple_of(code_ref[entry], HEAD)
                picked.append(win_ref[pl.ds(row, BS), :])
                targets.append(target_ref[entry])
            stack = jnp.concatenate(
                [
                    jnp.concatenate([picked[0], none], axis=1),
                    jnp.concatenate([none, picked[1]], axis=1),
                ],
                axis=0,
            )
            r = jnp.dot(blocks[i], stack, preferred_element_type=F32)
            r += jnp.dot(lows[i], stack, preferred_element_type=F32)
            acc_one[targets[0]] += r[:, : 2 * BS]
            acc_two[targets[1]] += r[:, 2 * BS :]
            return carry

        lax.fori_loop(0, SHARD, right, 0, unroll=SHARD)


def multiplied(codes, targets, win, blocks, lows):
    smem = pl.BlockSpec(memory_space=pltpu.SMEM)
    vmem = pl.BlockSpec(memory_space=pltpu.VMEM)
    return pl.pallas_call(
        right_kernel,
        out_shape=(pltpu.VMEM((ACCS, BS, 2 * BS), F32),) * SLOTS,
        in_specs=[smem, smem, vmem, vmem, vmem],
        out_specs=(vmem,) * SLOTS,
        compiler_params=pltpu.CompilerParams(vmem_limit_bytes=8 * 2**20),
        name="right_products",
    )(codes, targets, win, blocks, lows)


STEPS = ((2, 1), (1, 1), (3, 1), (0, 1), (2, 0), (1, 0), (3, 0))


def reduce_kernel(
    acc_one, acc_two, out_ref, part_ref, short_ref, landed, total, placed,
    send_sem, recv_sem, send2, recv2,
):
    b, g = lax.axis_index("blk"), lax.axis_index("grp")
    y, h = g // 2, g % 2
    others = [(y + dy) % CB * 2 + (h + dh) % 2 for dy, dh in STEPS]
    barrier = pltpu.get_barrier_semaphore()
    for other in others:
        pl.semaphore_signal(barrier, inc=1, device_id=(b, other), device_id_type=MESH)

    low = lax.broadcasted_iota(jnp.int32, (BS, 2 * BS), 1) < BS

    def fold(t, carry):
        one, two, three, four = (acc_one[4 * t + n] + acc_two[4 * t + n] for n in range(4))
        first = one + pltpu.roll(two, BS, 1)
        second = pltpu.roll(three, BS, 1) + four
        place = t % GROUP * SPAN + t // GROUP
        block = jnp.where(low, first, second)
        part_ref[place] = block
        short_ref[place] = block.astype(BF16)
        return carry

    lax.fori_loop(0, BLOCKS, fold, 0, unroll=8)
    pl.semaphore_wait(barrier, GROUP - 1)
    first = []
    for n, other in enumerate(others):
        copy = pltpu.make_async_remote_copy(
            src_ref=short_ref.at[pl.ds(other * SPAN, SPAN)],
            dst_ref=landed.at[n],
            send_sem=send_sem.at[n],
            recv_sem=recv_sem.at[n],
            device_id=(b, other),
            device_id_type=MESH,
        )
        copy.start()
        first.append(copy)
    out_ref[...] = jnp.zeros(out_ref.shape, F32)
    total[...] = part_ref[pl.ds(g * SPAN, SPAN)]
    for n, copy in enumerate(first):
        copy.wait_recv()
        total[...] += landed[n].astype(F32)

    def hop(d):
        panel = (b + PANELS - 2 + d) % PANELS
        owner, side = panel // 2, panel % 2
        copy = pltpu.make_async_remote_copy(
            src_ref=total.at[d],
            dst_ref=placed.at[side, g],
            send_sem=send2.at[d],
            recv_sem=recv2.at[side],
            device_id=(b, owner),
            device_id_type=MESH,
        )
        return owner, side, copy

    for d in range(SPAN):
        owner, side, copy = hop(d)

        @pl.when(owner != g)
        def _(copy=copy):
            copy.start()

        @pl.when(owner == g)
        def _(d=d, side=side):
            placed[side, g] = total[d]

    for side in range(2):
        d = (2 * g + side + PANELS + 2 - b) % PANELS

        @pl.when(d < SPAN)
        def _(side=side):
            rest = placed.at[side, pl.ds(0, GROUP - 1)]
            pltpu.make_async_remote_copy(
                src_ref=rest,
                dst_ref=rest,
                send_sem=send2.at[0],
                recv_sem=recv2.at[side],
                device_id=(b, others[0]),
                device_id_type=MESH,
            ).wait_recv()
            for n in range(GROUP):
                block = placed[side, n]
                row, column = side * CB + n // 2, n % 2 * 2
                out_ref[row, column] = block[:, :BS]
                out_ref[row, column + 1] = block[:, BS:]

    for d in range(SPAN):
        owner, side, copy = hop(d)

        @pl.when(owner != g)
        def _(copy=copy):
            copy.wait_send()

    for copy in first:
        copy.wait_send()


def reduced(acc_one, acc_two):
    vmem = pl.BlockSpec(memory_space=pltpu.VMEM)
    return pl.pallas_call(
        reduce_kernel,
        out_shape=jax.ShapeDtypeStruct((GROUP, CB, BS, BS), F32),
        in_specs=[vmem, vmem],
        out_specs=vmem,
        scratch_shapes=[
            pltpu.VMEM((BLOCKS, BS, 2 * BS), F32),
            pltpu.VMEM((BLOCKS, BS, 2 * BS), BF16),
            pltpu.VMEM((GROUP - 1, SPAN, BS, 2 * BS), BF16),
            pltpu.VMEM((SPAN, BS, 2 * BS), F32),
            pltpu.VMEM((2, GROUP, BS, 2 * BS), F32),
            pltpu.SemaphoreType.DMA((GROUP - 1,)),
            pltpu.SemaphoreType.DMA((GROUP - 1,)),
            pltpu.SemaphoreType.DMA((SPAN,)),
            pltpu.SemaphoreType.DMA((2,)),
        ],
        compiler_params=pltpu.CompilerParams(
            collective_id=1, has_side_effects=True, vmem_limit_bytes=12 * 2**20
        ),
        name="reduce_blocks",
    )(acc_one, acc_two)


def local(block_values, block_columns, row_counts, prolong_blocks, aggregates):
    win, blocks, lows, codes, targets = gathered(
        prolong_blocks,
        aggregates,
        block_columns.T,
        row_counts,
        jnp.transpose(block_values, (1, 2, 3, 0)),
    )
    win = win.reshape(-1, 2 * BS)
    return reduced(*multiplied(codes, targets, win, blocks, lows))


def solution(mesh):
    in_specs = (
        P("blk", "grp", None, None),
        P("blk", "grp"),
        P("blk"),
        P(("blk", "grp"), None, None),
        P(("blk", "grp")),
    )
    out_specs = P("grp", "blk", None, None)
    return jax.shard_map(local, mesh=mesh, in_specs=in_specs, out_specs=out_specs, check_vma=False)
```

```python
import functools

import jax
import jax.numpy as jnp
from jax import lax
from jax.experimental import pallas as pl
from jax.experimental.pallas import tpu as pltpu
from jax.sharding import PartitionSpec as P

MESH = pl.DeviceIdType.MESH
BF16, F32 = jnp.bfloat16, jnp.float32

BS = 64
CB = 4
ROWS = 384
SHARD = 48
PAIRS = SHARD // 2
PANELS = 16
GROUP = 8
SPAN = 5
HEAD = 16
LEN = HEAD + PAIRS * BS
CUT = HEAD + 13 * BS
F_PART, L_PART = (0, CUT), (CUT, LEN - CUT)
F_HALVES = ((0, 416), (416, CUT - 416))
L_HALVES = ((CUT, 352), (CUT + 352, 352))
SLOTS = 2
TARGETS = SPAN * CB * CB * 2
ACCS = TARGETS + 8
BLOCKS = TARGETS // 4
PITCH = 136


def turn(a_ref, turned, blocks, first):
    def over(r, carry):
        both = jnp.concatenate(
            [a_ref[s, r, :, first : first + 128] for s in range(SLOTS)], axis=0
        )
        start = pl.multiple_of(r * PITCH, 8)
        turned[pl.ds(start, 128), :] = both.T.astype(F32)
        return carry

    lax.fori_loop(0, BS, over, 0, unroll=16)

    def collect(i, carry):
        blocks[first + i] = turned[pl.ds(i, BS, stride=PITCH), :].astype(BF16)
        return carry

    lax.fori_loop(0, 128, collect, 0, unroll=16)


def left(win_ref, blocks, shard):
    def pair(j, carry):
        start = pl.multiple_of(HEAD + j * BS, HEAD)
        both = win_ref[2, shard, pl.ds(start, BS), :].T
        for half in range(2):
            i = shard * SHARD + 2 * j + half
            t = jnp.dot(
                both[half * BS : (half + 1) * BS, :], blocks[i], preferred_element_type=F32
            )
            blocks[i] = t.astype(BF16)
        return carry

    lax.fori_loop(0, PAIRS, pair, 0, unroll=12)


def gather_kernel(
    p_ref, agg_hbm, columns_hbm, counts_hbm, a_hbm,
    win_ref, blocks, code_ref, target_ref,
    raw, own, a_ref, turned, agg_ref, columns_ref, counts_ref, shards, withins,
    local_sem, send_sem, recv_sem,
):
    b, g = lax.axis_index("blk"), lax.axis_index("grp")
    core = b % 2
    y, h = g // 2, g % 2
    other = g + 1 - 2 * h
    z = (b // 2) % 4
    up_end = jnp.where(z == 3, 1, 0)
    down_end = jnp.where(z == 0, 1, 0)

    def on_k(step, end, dh):
        return (b + step + PANELS) % PANELS, g + dh * end * (1 - 2 * h)

    up_y, down_y = (b, (g + 2) % GROUP), (b, (g + GROUP - 2) % GROUP)
    across, sibling = (b, other), (b + 1 - 2 * core, g)

    load = pltpu.make_async_copy(p_ref, raw, local_sem.at[0])
    load.start()
    small = [
        pltpu.make_async_copy(source, target, local_sem.at[3 + n])
        for n, (source, target) in enumerate(
            ((agg_hbm, agg_ref), (columns_hbm, columns_ref), (counts_hbm, counts_ref))
        )
    ]
    for copy in small:
        copy.start()
    barrier = pltpu.get_barrier_semaphore()
    greeted = [up_y, down_y, across, sibling]
    for step in (2, PANELS - 2):
        greeted += [((b + step) % PANELS, column) for column in (g, other)]
    for device in greeted:
        pl.semaphore_signal(barrier, inc=1, device_id=device, device_id_type=MESH)
    small[0].wait()
    own[0:HEAD, :] = jnp.zeros((HEAD, 2 * BS), BF16)
    own[0:HEAD, 0:SHARD] = jnp.broadcast_to(
        (agg_ref[...] % CB).astype(F32).reshape(1, SHARD), (HEAD, SHARD)
    ).astype(BF16)
    load.wait()
    load_a = pltpu.make_async_copy(a_hbm, a_ref, local_sem.at[2])
    load_a.start()

    def pack(j, carry):
        row = pl.multiple_of(HEAD + j * BS, HEAD)
        own[pl.ds(row, BS), :] = jnp.concatenate([raw[2 * j], raw[2 * j + 1]], axis=-1)
        return carry

    lax.fori_loop(0, PAIRS, pack, 0, unroll=8)
    keep = pltpu.make_async_copy(own, win_ref.at[2, g], local_sem.at[1])
    keep.start()
    pl.semaphore_wait(barrier, len(greeted))

    copies, arrived, settled = {}, [], set()

    def at(d, dy, dh):
        return win_ref.at[d, ((y + dy) % 4) * 2 + (h + dh) % 2]

    def send(name, part, d, dy, dh, to_d, device, src=None):
        start, size = part
        piece = pl.ds(start, size)
        n = len(copies)
        source = own if src is not None else at(d, dy, dh)
        copies[name] = pltpu.make_async_remote_copy(
            src_ref=source.at[piece, :],
            dst_ref=at(to_d, dy, dh).at[piece, :],
            send_sem=send_sem.at[n],
            recv_sem=recv_sem.at[n],
            device_id=device,
            device_id_type=MESH,
        )
        copies[name].start()

    def got(*names):
        for name in names:
            copies[name].wait_recv()
            arrived.append(name)

    def settle():
        for name in arrived:
            if name not in settled:
                settled.add(name)
                copies[name].wait_send()

    def to_y(part, tag, d, dh, src=None):
        send((tag, "y+", d, dh), part, d, 0, dh, d, up_y, src)
        send((tag, "y-", d, dh), part, d, 0, dh, d, down_y, src)

    def on_y(halves, tag, d, dh):
        send((tag, "f+", d, dh), halves[0], d, -1, dh, d, up_y)
        send((tag, "f-", d, dh), halves[1], d, 1, dh, d, down_y)

    def to_z(part, tag, dy, dh, src=None):
        for sign, step, end, to_d in (("z+", 2, up_end, 0), ("z-", -2, down_end, 4)):
            column = dh * (1 - end)
            send((tag, sign, dy, dh), part, 2, dy, column, to_d, on_k(step, end, dh), src)

    def over(part, tag, dy, dh, src=None):
        send((tag, "s", dy, dh), part, 2, dy, dh, 1 + 2 * core, sibling, src)

    def over_far(part, tag, dy, dh):
        send((tag, "t", dy, dh), part, 4 - 4 * core, dy, dh, 3 - 2 * core, sibling)

    send(("F", "x"), F_PART, 2, 0, 0, 2, across, own)
    to_y(F_PART, "F", 2, 0, own)
    to_z(F_PART, "F", 0, 0, own)
    send(("L", "x"), L_PART, 2, 0, 0, 2, across, own)
    to_z(L_PART, "L", 0, 0, own)
    to_y(L_PART, "L", 2, 0, own)
    over((0, LEN), "A", 0, 0, own)

    for copy in small[1:]:
        copy.wait()
    loc = jnp.mod(columns_ref[...] - (b - 2) * ROWS, PANELS * ROWS)
    slot = g * SLOTS + lax.broadcasted_iota(jnp.int32, (SLOTS, ROWS), 0)
    live = slot < counts_ref[...].reshape(1, ROWS)
    shard, within = loc // SHARD, loc % SHARD
    row = jnp.where(live, shard * LEN + HEAD + within // 2 * BS, HEAD)
    shard = jnp.where(live, shard, SPAN * GROUP)
    for value, target in ((row, code_ref), (shard, shards), (within, withins)):
        target[...] = jnp.zeros((8, 128), jnp.int32)
        for c in range(ROWS // 128):
            target[2 * c : 2 * c + 2, :] = value[:, c * 128 : (c + 1) * 128]
    load_a.wait()
    turn(a_ref, turned, blocks, 0)
    got(("F", "x"))
    to_y(F_PART, "F", 2, 1)
    keep.wait()
    to_z(F_PART, "F", 0, 1)
    got(("F", "y+", 2, 0), ("F", "y-", 2, 0))
    on_y(F_HALVES, "F", 2, 0)
    for dy in (-1, 1):
        to_z(F_PART, "F", dy, 0)
    got(("L", "x"))
    to_z(L_PART, "L", 0, 1)
    to_y(L_PART, "L", 2, 1)
    over((0, LEN), "A", 0, 1)
    got(("L", "y+", 2, 0), ("L", "y-", 2, 0))
    on_y(L_HALVES, "L", 2, 0)
    for dy in (-1, 1):
        over((0, LEN), "A", dy, 0)
    got(("L", "z+", 0, 0), ("L", "z-", 0, 0))
    for d in (0, 4):
        to_y(L_PART, "L", d, 0)
    over_far(L_PART, "L", 0, 0)
    turn(a_ref, turned, blocks, 128)
    got(("F", "y+", 2, 1), ("F", "y-", 2, 1))
    on_y(F_HALVES, "F", 2, 1)
    for dy in (-1, 1):
        to_z(F_PART, "F", dy, 1)
    got(("F", "f+", 2, 0), ("F", "f-", 2, 0))
    to_z(F_PART, "F", 2, 0)
    got(("L", "z+", 0, 1), ("L", "z-", 0, 1))
    for d in (0, 4):
        to_y(L_PART, "L", d, 1)
    over_far(L_PART, "L", 0, 1)
    got(("F", "f+", 2, 1), ("F", "f-", 2, 1))
    to_z(F_PART, "F", 2, 1)
    got(("L", "y+", 2, 1), ("L", "y-", 2, 1))
    on_y(L_HALVES, "L", 2, 1)
    for dy in (-1, 1):
        over((0, LEN), "A", dy, 1)
    turn(a_ref, turned, blocks, 256)
    got(("L", "f+", 2, 0), ("L", "f-", 2, 0))
    over((0, LEN), "A", 2, 0)
    got(("F", "z+", 0, 0), ("F", "z-", 0, 0))
    over_far(F_PART, "F", 0, 0)
    for d in (0, 4):
        got(("L", "y+", d, 0), ("L", "y-", d, 0))
        on_y(L_HALVES, "L", d, 0)
    for dy in (-1, 1):
        over_far(L_PART, "L", dy, 0)
    got(("L", "f+", 2, 1), ("L", "f-", 2, 1))
    over((0, LEN), "A", 2, 1)
    for shard in range(0, 2):
        left(win_ref, blocks, shard)
    got(("F", "z+", 0, 1), ("F", "z-", 0, 1))
    over_far(F_PART, "F", 0, 1)
    for dy in (-1, 1):
        got(("F", "z+", dy, 0), ("F", "z-", dy, 0))
        over_far(F_PART, "F", dy, 0)
        left(win_ref, blocks, 2 + (dy + 1) // 2)
    for d in (0, 4):
        got(("L", "y+", d, 1), ("L", "y-", d, 1))
        on_y(L_HALVES, "L", d, 1)
    for dy in (-1, 1):
        over_far(L_PART, "L", dy, 1)
    for n, (dy, dh) in enumerate(((-1, 1), (1, 1), (2, 0), (2, 1))):
        left(win_ref, blocks, 4 + n)
        settle()
        got(("F", "z+", dy, dh), ("F", "z-", dy, dh))
        over_far(F_PART, "F", dy, dh)
    for dh in (0, 1):
        for d in (0, 4):
            got(("L", "f+", d, dh), ("L", "f-", d, dh))
        over_far(L_PART, "L", 2, dh)
    for name in copies:
        if name[1] in ("s", "t"):
            got(name)
    for name in copies:
        if name not in settled:
            copies[name].wait_send()

    place = lax.broadcasted_iota(jnp.int32, (8, 128), 0) // 2 * 128
    place += lax.broadcasted_iota(jnp.int32, (8, 128), 1)
    shard, within = shards[...], withins[...]
    target = jnp.full((8, 128), TARGETS, jnp.int32)
    column = jnp.zeros((8, 128), jnp.int32)

    def look(value, index):
        table = jnp.broadcast_to(value, (8, 128))
        return jnp.take_along_axis(table, index, axis=1, mode="promise_in_bounds")

    for n in range(SPAN * GROUP):
        d = n // GROUP
        near = win_ref[d, n % GROUP, 0:HEAD, :].astype(F32)[0:1].astype(jnp.int32)
        found = look((near + d * CB) * (2 * CB), within)
        target = jnp.where(shard == n, found, target)
        if d == 2:
            found = look(near * 2, place % SHARD)
            column = jnp.where(place // SHARD == n % GROUP, found, column)
    target_ref[...] = target + column + within % 2


COPIES = 86 - 8


def gathered(prolong, aggs, columns, counts, a):
    vmem, hbm = pl.BlockSpec(memory_space=pltpu.VMEM), pl.BlockSpec(memory_space=pltpu.HBM)
    return pl.pallas_call(
        gather_kernel,
        out_shape=(
            pltpu.VMEM((SPAN, GROUP, LEN, 2 * BS), BF16),
            pltpu.VMEM((ROWS, BS, 2 * BS), BF16),
            jax.ShapeDtypeStruct((8, 128), jnp.int32),
            jax.ShapeDtypeStruct((8, 128), jnp.int32),
        ),
        in_specs=[hbm] * 5,
        out_specs=(vmem, vmem, vmem, vmem),
        scratch_shapes=[
            pltpu.VMEM((SHARD, BS, BS), BF16),
            pltpu.VMEM((LEN, 2 * BS), BF16),
            pltpu.VMEM((SLOTS, BS, BS, ROWS), BF16),
            pltpu.VMEM((BS * PITCH, 128), F32),
            pltpu.VMEM((SHARD,), jnp.int32),
            pltpu.VMEM((SLOTS, ROWS), jnp.int32),
            pltpu.VMEM((ROWS,), jnp.int32),
            pltpu.VMEM((8, 128), jnp.int32),
            pltpu.VMEM((8, 128), jnp.int32),
            pltpu.SemaphoreType.DMA((6,)),
            pltpu.SemaphoreType.DMA((COPIES,)),
            pltpu.SemaphoreType.DMA((COPIES,)),
        ],
        compiler_params=pltpu.CompilerParams(
            collective_id=0, has_side_effects=True, vmem_limit_bytes=20 * 2**20
        ),
        name="gather_window",
    )(*(pltpu.with_memory_space_constraint(x, pltpu.HBM) for x in (prolong, aggs, columns, counts, a)))


def right_kernel(code_ref, target_ref, win_ref, blocks, acc_one, acc_two):
    def clear(t, carry):
        acc_one[t] = jnp.zeros((BS, 2 * BS), F32)
        acc_two[t] = jnp.zeros((BS, 2 * BS), F32)
        return carry

    lax.fori_loop(0, ACCS, clear, 0, unroll=8)

    for shard in range(GROUP):

        def right(j, carry, shard=shard):
            i = shard * SHARD + j
            none = jnp.zeros((BS, 2 * BS), BF16)
            targets, picked = [], []
            for s in range(SLOTS):
                entry = i // 128 * 2 + s, i % 128
                row = pl.multiple_of(code_ref[entry], HEAD)
                picked.append(win_ref[pl.ds(row, BS), :])
                targets.append(target_ref[entry])
            stack = jnp.concatenate(
                [
                    jnp.concatenate([picked[0], none], axis=1),
                    jnp.concatenate([none, picked[1]], axis=1),
                ],
                axis=0,
            )
            r = jnp.dot(blocks[i], stack, preferred_element_type=F32)
            acc_one[targets[0]] += r[:, : 2 * BS]
            acc_two[targets[1]] += r[:, 2 * BS :]
            return carry

        lax.fori_loop(0, SHARD, right, 0, unroll=SHARD)


def multiplied(codes, targets, win, blocks):
    smem = pl.BlockSpec(memory_space=pltpu.SMEM)
    vmem = pl.BlockSpec(memory_space=pltpu.VMEM)
    return pl.pallas_call(
        right_kernel,
        out_shape=(pltpu.VMEM((ACCS, BS, 2 * BS), F32),) * SLOTS,
        in_specs=[smem, smem, vmem, vmem],
        out_specs=(vmem,) * SLOTS,
        compiler_params=pltpu.CompilerParams(vmem_limit_bytes=8 * 2**20),
        name="right_products",
    )(codes, targets, win, blocks)


STEPS = ((2, 1, 1), (1, 1, 1), (3, 1, 1), (0, 1, 0), (2, 0, 1), (1, 0, 0), (3, 0, 0))


def reduce_kernel(
    acc_one, acc_two, out_ref, part_ref, short_ref, landed, landed_short, total, placed,
    send_sem, recv_sem, send2, recv2,
):
    b, g = lax.axis_index("blk"), lax.axis_index("grp")
    y, h = g // 2, g % 2
    others = [(y + dy) % CB * 2 + (h + dh) % 2 for dy, dh, _ in STEPS]
    barrier = pltpu.get_barrier_semaphore()
    for other in others:
        pl.semaphore_signal(barrier, inc=1, device_id=(b, other), device_id_type=MESH)

    low = lax.broadcasted_iota(jnp.int32, (BS, 2 * BS), 1) < BS

    def fold(t, carry):
        one, two, three, four = (acc_one[4 * t + n] + acc_two[4 * t + n] for n in range(4))
        first = one + pltpu.roll(two, BS, 1)
        second = pltpu.roll(three, BS, 1) + four
        place = t % GROUP * SPAN + t // GROUP
        block = jnp.where(low, first, second)
        part_ref[place] = block
        short_ref[place] = block.astype(BF16)
        return carry

    lax.fori_loop(0, BLOCKS, fold, 0, unroll=8)
    pl.semaphore_wait(barrier, GROUP - 1)
    first, places = [], []
    for n, (other, (dy, dh, short)) in enumerate(zip(others, STEPS)):
        source, target = (short_ref, landed_short) if short else (part_ref, landed)
        place = target.at[sum(step[2] == short for step in STEPS[:n])]
        copy = pltpu.make_async_remote_copy(
            src_ref=source.at[pl.ds(other * SPAN, SPAN)],
            dst_ref=place,
            send_sem=send_sem.at[n],
            recv_sem=recv_sem.at[n],
            device_id=(b, other),
            device_id_type=MESH,
        )
        copy.start()
        first.append(copy)
        places.append(place)
    out_ref[...] = jnp.zeros(out_ref.shape, F32)
    total[...] = part_ref[pl.ds(g * SPAN, SPAN)]
    for copy, place in zip(first, places):
        copy.wait_recv()
        total[...] += place[...].astype(F32)

    def hop(d):
        panel = (b + PANELS - 2 + d) % PANELS
        owner, side = panel // 2, panel % 2
        copy = pltpu.make_async_remote_copy(
            src_ref=total.at[d],
            dst_ref=placed.at[side, g],
            send_sem=send2.at[d],
            recv_sem=recv2.at[side],
            device_id=(b, owner),
            device_id_type=MESH,
        )
        return owner, side, copy

    for d in range(SPAN):
        owner, side, copy = hop(d)

        @pl.when(owner != g)
        def _(copy=copy):
            copy.start()

        @pl.when(owner == g)
        def _(d=d, side=side):
            placed[side, g] = total[d]

    for side in range(2):
        d = (2 * g + side + PANELS + 2 - b) % PANELS

        @pl.when(d < SPAN)
        def _(side=side):
            rest = placed.at[side, pl.ds(0, GROUP - 1)]
            pltpu.make_async_remote_copy(
                src_ref=rest,
                dst_ref=rest,
                send_sem=send2.at[0],
                recv_sem=recv2.at[side],
                device_id=(b, others[0]),
                device_id_type=MESH,
            ).wait_recv()
            for n in range(GROUP):
                block = placed[side, n]
                row, column = side * CB + n // 2, n % 2 * 2
                out_ref[row, column] = block[:, :BS]
                out_ref[row, column + 1] = block[:, BS:]

    for d in range(SPAN):
        owner, side, copy = hop(d)

        @pl.when(owner != g)
        def _(copy=copy):
            copy.wait_send()

    for copy in first:
        copy.wait_send()


def reduced(acc_one, acc_two):
    vmem = pl.BlockSpec(memory_space=pltpu.VMEM)
    return pl.pallas_call(
        reduce_kernel,
        out_shape=jax.ShapeDtypeStruct((GROUP, CB, BS, BS), F32),
        in_specs=[vmem, vmem],
        out_specs=vmem,
        scratch_shapes=[
            pltpu.VMEM((BLOCKS, BS, 2 * BS), F32),
            pltpu.VMEM((BLOCKS, BS, 2 * BS), BF16),
            pltpu.VMEM((GROUP // 2 - 1, SPAN, BS, 2 * BS), F32),
            pltpu.VMEM((GROUP // 2, SPAN, BS, 2 * BS), BF16),
            pltpu.VMEM((SPAN, BS, 2 * BS), F32),
            pltpu.VMEM((2, GROUP, BS, 2 * BS), F32),
            pltpu.SemaphoreType.DMA((GROUP - 1,)),
            pltpu.SemaphoreType.DMA((GROUP - 1,)),
            pltpu.SemaphoreType.DMA((SPAN,)),
            pltpu.SemaphoreType.DMA((2,)),
        ],
        compiler_params=pltpu.CompilerParams(
            collective_id=1, has_side_effects=True, vmem_limit_bytes=12 * 2**20
        ),
        name="reduce_blocks",
    )(acc_one, acc_two)


def local(block_values, block_columns, row_counts, prolong_blocks, aggregates):
    win, blocks, codes, targets = gathered(
        prolong_blocks,
        aggregates,
        block_columns.T,
        row_counts,
        jnp.transpose(block_values, (1, 2, 3, 0)),
    )
    win = win.reshape(-1, 2 * BS)
    return reduced(*multiplied(codes, targets, win, blocks))


def solution(mesh):
    in_specs = (
        P("blk", "grp", None, None),
        P("blk", "grp"),
        P("blk"),
        P(("blk", "grp"), None, None),
        P(("blk", "grp")),
    )
    out_specs = P("grp", "blk", None, None)
    return jax.shard_map(local, mesh=mesh, in_specs=in_specs, out_specs=out_specs, check_vma=False)
```
